128 devices in a mesh: row: 8 (over y, x_lo), col: 16 (over x_hi, z, core).
Axes of the slice: x: 4 (x_hi: 2, x_lo: 2; x = x_hi * 2 + x_lo), y: 4, z: 4, core: 2. Of those that a mesh axis runs over, the one named last changes fastest.
Arguments:
- tokens: bfloat16 [128, 512, 512], P('row', 'col'), may hold values from -6 to 6
- norm_gain: float32 [512], replicated, may hold values from 0.1 to 1.9
- w_qkv: bfloat16 [512, 1536], replicated, may hold values from -0.25 to 0.25
- w_out: bfloat16 [512, 512], replicated, may hold values from -0.25 to 0.25
- head_scale: float32 [8], replicated, may hold values from 2 to 12
- cotangent: bfloat16 [128, 512, 512], P('row', 'col'), may hold values from -6 to 6
Outputs:
- layer_out: bfloat16 [128, 512, 512], P('row', 'col')
- d_tokens: bfloat16 [128, 512, 512], P('row', 'col')
- d_gain: float32 [512], replicated
- d_head_scale: float32 [8], replicated
- d_w_qkv: float32 [512, 1536], P('col', 'row')
- d_w_out: float32 [512, 512], P('col', 'row')
The draws below stay inside these ranges and needn't reach their ends.
All inputs are finite; a program needn't handle non-finite values.
Results may differ from the reference program's by a relative error of at most 0.025.
Values may be sent and summed in bfloat16 or wider, within the bound.
No kernel may reach another device: no remote copies, remote signals or barrier semaphores. Data moves between devices by JAX's collectives and lax.ppermute only.
A program may use at most 128 MiB of HBM per device.

```python
import math
import jax
import jax.numpy as jnp
from jax import lax

WIDTH = 512
HEAD = 64
HEADS = 8
WINDOW = 7
IMG_ROWS = 128
IMG_COLS = 512


def spiked(values, own_key, source, target, parts, factor):
    owner, partner = [(jnp.arange(values.shape[dim]) // (values.shape[dim] // parts)).reshape([-1 if axis == dim else 1 for axis in range(values.ndim)]) for dim in (source, target)]
    chosen = jax.random.permutation(own_key, parts)[partner]
    strong = (owner == chosen) | (owner == (partner + parts // 2) % parts)
    return jnp.where(strong, factor * values, values)


def level_of(stream_key, shape, cuts, least, high):
    factor_of = 1.0
    for dim, blocks in cuts:
        draws = jax.random.uniform(jax.random.fold_in(jax.random.fold_in(stream_key, 6), dim), (blocks,), jnp.float32, least / len(cuts), high / len(cuts))
        factor_of = factor_of * jnp.repeat(jnp.exp(draws), shape[dim] // blocks).reshape((-1,) + (1,) * (len(shape) - 1 - dim))
    return factor_of


def noise(own_key, extent, scale, limit, split=(), held_as=jnp.bfloat16):
    gain = level_of(own_key, extent, split, -0.22, 0.18) if split else 1.0
    values = jax.random.normal(own_key, extent, jnp.float32) * scale * gain
    return jnp.minimum(jnp.maximum(values, -limit), limit).astype(held_as)


def bell_draw_with(key, shape, spread, reach, pieces, heavy, kind=jnp.bfloat16):
    values = spread * jax.random.normal(key, shape, jnp.float32)
    if pieces:
        values = values * level_of(key, shape, pieces, -0.22, 0.18)
    return jnp.clip(spiked(values, jax.random.fold_in(key, 3), *heavy), -reach, reach).astype(kind)


def setup_inputs(seed: int = 0) -> dict:
    key_list = jax.random.split(jax.random.key(seed), 7)
    tokens = noise(key_list[0], (IMG_ROWS, IMG_COLS, WIDTH), 1.0, 6.0, ((0, 8), (1, 16)))
    norm_gain = jnp.clip(1.0 + 0.18 * jax.random.normal(key_list[1], (WIDTH,), jnp.float32), 0.1, 1.9)
    w_qkv = noise(key_list[2], (WIDTH, 3 * WIDTH), WIDTH ** -0.5, 0.25)
    w_out = noise(key_list[3], (WIDTH, WIDTH), WIDTH ** -0.5, 0.25)
    head_scale = jnp.clip(jnp.exp(jax.random.uniform(key_list[4], (HEADS,), jnp.float32, math.log(2.0), math.log(12.0))), 2.0, 12.0)
    cotangent = bell_draw_with(key_list[5], (IMG_ROWS, IMG_COLS, WIDTH), 1.0, 6.0, ((0, 8), (1, 16)), (0, 2, 8, 2.0))
    return {"tokens": tokens, "norm_gain": norm_gain, "w_qkv": w_qkv, "w_out": w_out, "head_scale": head_scale, "cotangent": cotangent}


EPS = 1e-06

def rms_gain(values, norm_gain):
    return values * lax.rsqrt(lax.optimization_barrier(jnp.mean(values * values, axis=-1, keepdims=True)) + EPS) * norm_gain

def unit_heads(values):
    shaped = values.reshape(values.shape[:-1] + (HEADS, HEAD))
    shaped = shaped * lax.rsqrt(lax.optimization_barrier(jnp.mean(shaped * shaped, axis=-1, keepdims=True)) + EPS)
    return shaped.reshape(values.shape)

def head_prep(qkv):
    width = qkv.shape[-1] // 3
    query = unit_heads(qkv[:, :width])
    keys = unit_heads(qkv[:, width:2 * width])
    return (query.astype(jnp.bfloat16), keys.astype(jnp.bfloat16), qkv[:, 2 * width:].astype(jnp.bfloat16))

def tile_attend(query, key_pad, value_pad, head_scale, row_start, col_start, total_rows, total_cols, block_rows, block_cols):
    row_count, col_count, width = query.shape
    margin = WINDOW // 2
    pad_rows = block_rows + 2 * margin
    pad_cols = block_cols + 2 * margin
    across = col_count // block_cols
    count = row_count // block_rows * across
    q_pos = jnp.arange(block_rows * block_cols, dtype=jnp.int32)
    q_row = q_pos // block_cols
    q_col = q_pos % block_cols
    k_pos = jnp.arange(pad_rows * pad_cols, dtype=jnp.int32)
    k_row = k_pos // pad_cols
    k_col = k_pos % pad_cols
    row_diff = k_row[None, :] - q_row[:, None]
    col_diff = k_col[None, :] - q_col[:, None]
    near = (row_diff >= 0) & (row_diff < WINDOW) & (col_diff >= 0) & (col_diff < WINDOW)
    scale_row = (head_scale / HEAD)[:, None, None]

    def one_block(block_id):
        top = block_id // across * block_rows
        left = block_id % across * block_cols
        q_blk = lax.dynamic_slice(query, (top, left, jnp.int32(0)), (block_rows, block_cols, width))
        k_blk = lax.dynamic_slice(key_pad, (top, left, jnp.int32(0)), (pad_rows, pad_cols, width))
        v_blk = lax.dynamic_slice(value_pad, (top, left, jnp.int32(0)), (pad_rows, pad_cols, width))
        q_blk = q_blk.reshape(block_rows * block_cols, HEADS, HEAD)
        k_blk = k_blk.reshape(pad_rows * pad_cols, HEADS, HEAD)
        v_blk = v_blk.reshape(pad_rows * pad_cols, HEADS, HEAD)
        key_row = row_start + top + k_row - margin
        key_col = col_start + left + k_col - margin
        inside = (key_row >= 0) & (key_row < total_rows) & (key_col >= 0) & (key_col < total_cols)
        valid = near & inside[None, :]
        score = jnp.einsum('qhd,khd->hqk', q_blk, k_blk, precision=lax.Precision.HIGHEST) * scale_row
        weight = jnp.where(valid[None], jnp.exp(score), jnp.float32(0.0)).astype(jnp.bfloat16)
        weight = lax.optimization_barrier(weight).astype(jnp.float32)
        numer = jnp.einsum('hqk,khd->qhd', weight, v_blk, precision=lax.Precision.HIGHEST)
        denom = lax.optimization_barrier(jnp.sum(weight, axis=-1)).T
        out = numer / denom[:, :, None]
        return out.reshape(block_rows, block_cols, width).astype(jnp.bfloat16)
    blocks = lax.map(jax.checkpoint(one_block), jnp.arange(count, dtype=jnp.int32))
    blocks = blocks.reshape(row_count // block_rows, across, block_rows, block_cols, width)
    return blocks.transpose(0, 2, 1, 3, 4).reshape(row_count, col_count, width)

def reference(tokens, norm_gain, w_qkv, w_out, head_scale, cotangent):
    row_count, col_count, width = tokens.shape
    tok_count = row_count * col_count
    margin = WINDOW // 2
    normed, norm_pull = jax.vjp(rms_gain, tokens.astype(jnp.float32), norm_gain)
    normed_b = normed.astype(jnp.bfloat16).reshape(tok_count, width)
    qkv = jnp.dot(normed_b, w_qkv, preferred_element_type=jnp.float32)
    (query, keys, values), prep_pull = jax.vjp(head_prep, qkv)
    grid_shape = (row_count, col_count, width)
    pad_spec = ((margin, margin), (margin, margin), (0, 0))
    key_pad = jnp.pad(keys.reshape(grid_shape).astype(jnp.float32), pad_spec)
    value_pad = jnp.pad(values.reshape(grid_shape).astype(jnp.float32), pad_spec)
    block_rows = min(row_count, 8)
    block_cols = min(col_count, 16)

    def local_attend(q_in, k_in, v_in, scale_in):
        return tile_attend(q_in, k_in, v_in, scale_in, 0, 0, row_count, col_count, block_rows, block_cols)
    attn, attend_pull = jax.vjp(local_attend, query.reshape(grid_shape).astype(jnp.float32), key_pad, value_pad, head_scale)
    attn_flat = attn.reshape(tok_count, width)
    mixed = jnp.dot(attn_flat, w_out, preferred_element_type=jnp.float32).reshape(grid_shape)
    layer_out = (tokens.astype(jnp.float32) + mixed).astype(jnp.bfloat16)
    cot_flat = cotangent.reshape(tok_count, width)
    d_attn = jnp.dot(cot_flat, w_out.T, preferred_element_type=jnp.float32).astype(jnp.bfloat16)
    d_w_out = jnp.dot(attn_flat.T, cot_flat, preferred_element_type=jnp.float32)
    d_query, d_key_pad, d_value_pad, d_scale = attend_pull(d_attn.reshape(grid_shape))
    d_query_b = d_query.astype(jnp.bfloat16)
    d_keys = d_key_pad[margin:margin + row_count, margin:margin + col_count].astype(jnp.bfloat16)
    d_values = d_value_pad[margin:margin + row_count, margin:margin + col_count].astype(jnp.bfloat16)
    d_qkv, = prep_pull((d_query_b.reshape(tok_count, width), d_keys.reshape(tok_count, width), d_values.reshape(tok_count, width)))
    d_qkv_b = d_qkv.astype(jnp.bfloat16)
    d_w_qkv = jnp.dot(normed_b.T, d_qkv_b, preferred_element_type=jnp.float32)
    d_normed = jnp.dot(d_qkv_b, w_qkv.T, preferred_element_type=jnp.float32).reshape(grid_shape)
    d_input, d_gain = norm_pull(d_normed)
    d_tokens = (cotangent.astype(jnp.float32) + d_input).astype(jnp.bfloat16)
    factor = jnp.float32(1.0) / jnp.sqrt(jnp.float32(tok_count))
    return (layer_out, d_tokens, d_gain * factor, d_scale * factor, d_w_qkv * factor, d_w_out * factor)
```

```python
import math

import jax
import jax.numpy as jnp
import numpy as np
from jax import lax
from jax.experimental import pallas as pl
from jax.experimental.pallas import tpu as pltpu
from jax.sharding import Mesh
from jax.sharding import PartitionSpec as P

HEAD = 64
HEADS = 8
WINDOW = 7
WIDTH = 512
EPS = 1e-06

MARGIN = WINDOW // 2
ROWS, COLS = 16, 32
SIDE = 4
PITCH = COLS + 2 * SIDE
EXT_ROWS = ROWS + 2 * MARGIN
EXT = EXT_ROWS * PITCH
EXT_PAD = -(-EXT // 128) * 128
BLOCK_ROWS = 4
BLOCKS = ROWS // BLOCK_ROWS
QUERIES = BLOCK_ROWS * COLS
KEY_ROWS = BLOCK_ROWS + 2 * MARGIN
KEYS = KEY_ROWS * PITCH
STEP = BLOCK_ROWS * PITCH
PAIR = 2 * HEAD
PAIRS = HEADS // 2
FAR = -1.0e4
LOG2E = math.log2(math.e)
LN2 = math.log(2.0)

F32 = jnp.float32
BF16 = jnp.bfloat16


def mm(a, b):
    return lax.dot_general(a, b, (((1,), (0,)), ((), ())), preferred_element_type=F32)


def mm_nt(a, b):
    return lax.dot_general(a, b, (((1,), (1,)), ((), ())), preferred_element_type=F32)


def mm_tn(a, b):
    return lax.dot_general(a, b, (((0,), (0,)), ((), ())), preferred_element_type=F32)


def split_two(v):
    high = v.astype(BF16)
    return high, (v - high.astype(F32)).astype(BF16)


def head_mean(v, ones):
    high, low = split_two(v)
    return mm(jnp.concatenate([high, low], axis=1), ones)


def layer_kernel(
    scale_ref, ctr, side, cot, gain, w_qkv, w_out, k_mask, q_mask, ones_ref,
    layer_out, d_ctr, d_side, d_w, small,
    xhat, inv_rms, nb, nb_t, d_norm, raw, k_hat, k_inv, kb, vb, d_kv, d_raw, attn, attn_t,
):
    pair = pl.program_id(0)
    at = lambda base: pl.ds(pl.multiple_of(base + pair * PAIR, PAIR), PAIR)

    @pl.when(pair == 0)
    def _():
        xhat[EXT:, :] = jnp.zeros((EXT_PAD - EXT, WIDTH), F32)
        for r in range(EXT_ROWS):
            xhat[r * PITCH : r * PITCH + COLS, :] = ctr[r].astype(F32)
            xhat[r * PITCH + COLS : (r + 1) * PITCH, :] = side[r].astype(F32)
        for top in range(0, EXT_PAD, 128):
            rows = slice(top, top + 128)
            x = xhat[rows, :]
            inv = lax.rsqrt(jnp.mean(x * x, axis=-1, keepdims=True) + EPS)
            x = x * inv
            xhat[rows, :] = x
            inv_rms[rows, :] = inv
            normed = (x * gain[...]).astype(BF16)
            nb[rows, :] = normed
            nb_t[:, rows] = normed.T
            d_norm[rows, :] = jnp.zeros((128, WIDTH), F32)
        small[...] = jnp.zeros((8, WIDTH), F32)

    ones = ones_ref[...]
    w_pair = jnp.concatenate([w_qkv[:, at(0)], w_qkv[:, at(WIDTH)], w_qkv[:, at(2 * WIDTH)]], axis=1)
    raw[...] = mm(nb[...], w_pair)
    k_raw = raw[:, PAIR : 2 * PAIR]
    inv = lax.rsqrt(head_mean(k_raw * k_raw, ones) + EPS)
    k_inv[...] = inv
    k_hat[...] = k_raw * inv
    kb[...] = (k_raw * inv).astype(BF16)
    vb[...] = raw[:, 2 * PAIR :].astype(BF16)
    own = [(MARGIN + r) * PITCH for r in range(ROWS)]
    q_raw = jnp.concatenate([raw[o : o + COLS, 0:PAIR] for o in own], axis=0)
    q_inv = lax.rsqrt(head_mean(q_raw * q_raw, ones) + EPS)
    q_hat = q_raw * q_inv
    lane = lax.broadcasted_iota(jnp.int32, (1, PAIR), 1)
    scale = jnp.where(lane < HEAD, scale_ref[2 * pair], scale_ref[2 * pair + 1])
    q_scaled = q_hat * (scale * (LOG2E / HEAD))
    d_attn_t = mm_nt(w_out[at(0), :], cot[...]).astype(BF16)
    first_rows = lax.broadcasted_iota(jnp.int32, (PAIR, QUERIES), 0) < HEAD
    first_lanes = lax.broadcasted_iota(jnp.int32, (QUERIES, PAIR), 1) < HEAD
    d_kv[...] = jnp.zeros((EXT_PAD, 2 * PAIR), F32)

    def beside(v):
        return jnp.concatenate(
            [jnp.where(first_rows, v, 0.0), jnp.where(first_rows, 0.0, v)], axis=1
        ).astype(BF16)

    def above(v):
        return jnp.concatenate(
            [jnp.where(first_lanes, v, 0.0), jnp.where(first_lanes, 0.0, v)], axis=0
        ).astype(BF16)

    def diagonal(v):
        return jnp.concatenate([v[:HEAD, :QUERIES], v[HEAD:, QUERIES:]], axis=0)

    def spread(v):
        return jnp.where(first_rows, v[:, :QUERIES], v[:, QUERIES:])

    d_q_parts = []
    for b in range(BLOCKS):
        keys = kb[b * STEP : b * STEP + KEYS, :]
        values = vb[b * STEP : b * STEP + KEYS, :]
        q_nat = q_scaled[b * QUERIES : (b + 1) * QUERIES, :]
        q_all = jnp.concatenate([beside(q_nat.T), q_mask[...]], axis=0)
        weight = jnp.exp2(mm(jnp.concatenate([keys, k_mask[b]], axis=1), q_all))
        weight_b = weight.astype(BF16)
        inv_den = 1.0 / jnp.sum(weight_b.astype(F32), axis=0, keepdims=True)
        inv_den = spread(inv_den)
        out_t = diagonal(mm_tn(values, weight_b)) * inv_den
        attn_t[at(0), b * QUERIES : (b + 1) * QUERIES] = out_t.astype(BF16)
        attn[b * QUERIES : (b + 1) * QUERIES, at(0)] = out_t.T.astype(BF16)
        d_out_t = d_attn_t[:, b * QUERIES : (b + 1) * QUERIES].astype(F32) * inv_den
        dot_t = d_out_t * out_t
        delta = jnp.concatenate(
            [jnp.sum(dot_t[:HEAD], axis=0, keepdims=True), jnp.sum(dot_t[HEAD:], axis=0, keepdims=True)],
            axis=1,
        )
        d_weight = mm(values, beside(d_out_t))
        d_score = (weight * (d_weight - delta)).astype(BF16)
        d_values = mm(weight_b, above(d_out_t.T))
        d_keys = mm(d_score, above(q_nat))
        d_q_parts.append(diagonal(mm_tn(keys, d_score)).T)
        d_kv[b * STEP : b * STEP + KEYS, 0:PAIR] += d_keys
        d_kv[b * STEP : b * STEP + KEYS, PAIR:] += d_values

    d_q = jnp.concatenate(d_q_parts, axis=0) * (scale * (1.0 / HEAD))
    dot_q = q_hat * d_q
    by_lane = jnp.sum(dot_q, axis=0, keepdims=True) / scale
    first = jnp.sum(jnp.where(lane < HEAD, by_lane, 0.0), axis=1, keepdims=True)
    second = jnp.sum(jnp.where(lane < HEAD, 0.0, by_lane), axis=1, keepdims=True)
    spot = lax.broadcasted_iota(jnp.int32, (1, WIDTH), 1)
    small[1:2, :] += jnp.where(spot == 2 * pair, first, 0.0) + jnp.where(spot == 2 * pair + 1, second, 0.0)
    d_q_raw = q_inv * (d_q - q_hat * head_mean(dot_q, ones))
    d_raw[:, 0:PAIR] = jnp.zeros((EXT_PAD, PAIR), F32)
    for r, o in enumerate(own):
        d_raw[o : o + COLS, 0:PAIR] = d_q_raw[r * COLS : (r + 1) * COLS, :]
    d_k = d_kv[:, 0:PAIR] * LN2
    k_h = k_hat[...]
    d_raw[:, PAIR : 2 * PAIR] = k_inv[...] * (d_k - k_h * head_mean(k_h * d_k, ones))
    d_raw[:, 2 * PAIR :] = d_kv[:, PAIR:]
    d_raw_b = d_raw[...].astype(BF16)
    d_w_pair = mm(nb_t[...], d_raw_b).astype(BF16)
    for part in range(3):
        d_w[:, at(part * WIDTH)] = d_w_pair[:, part * PAIR : (part + 1) * PAIR]
    d_norm[...] += mm_nt(d_raw_b, w_pair)

    @pl.when(pair == PAIRS - 1)
    def _():
        mixed = mm(attn[...], w_out[...])
        for r in range(ROWS):
            layer_out[r] = (ctr[MARGIN + r].astype(F32) + mixed[r * COLS : (r + 1) * COLS, :]).astype(BF16)
        d_w[:, 3 * WIDTH :] = mm(attn_t[...], cot[...]).astype(BF16)
        d_gain = jnp.zeros((1, WIDTH), F32)
        for r in range(EXT_ROWS):
            rows = slice(r * PITCH, (r + 1) * PITCH)
            d_n = d_norm[rows, :]
            x = xhat[rows, :]
            d_gain += jnp.sum(x * d_n, axis=0, keepdims=True)
            d_n = d_n * gain[...]
            d_x = inv_rms[rows, :] * (d_n - x * jnp.mean(x * d_n, axis=-1, keepdims=True))
            d_ctr[r] = d_x[:COLS]
            d_side[r] = d_x[COLS:].astype(BF16)
        small[0:1, :] = d_gain


def masks(row_start, col_start, total_rows, total_cols):
    key = np.arange(KEYS)
    k_row, k_col = key // PITCH, key % PITCH
    k_col = np.where(k_col < COLS + SIDE, k_col, k_col - PITCH)
    near_col = np.abs(k_col[:, None] - np.arange(COLS)[None]) <= MARGIN
    ahead = k_row[:, None] - np.arange(BLOCK_ROWS)[None]
    near_row = (ahead >= 0) & (ahead < WINDOW)
    fixed = np.zeros((KEYS, 128), np.float32)
    fixed[:, :COLS] = np.where(near_col, 0.0, FAR)
    fixed[:, COLS : COLS + BLOCK_ROWS] = np.where(near_row, 0.0, FAR)
    row = row_start + np.arange(BLOCKS)[:, None] * BLOCK_ROWS + k_row[None] - MARGIN
    col = col_start + k_col[None]
    inside = (row >= 0) & (row < total_rows) & (col >= 0) & (col < total_cols)
    outside = jnp.where(inside, 0.0, FAR)[:, :, None]
    k_mask = jnp.where(np.arange(128) == COLS + BLOCK_ROWS, outside, fixed[None]).astype(BF16)
    query = np.arange(2 * QUERIES) % QUERIES
    q_mask = np.zeros((128, 2 * QUERIES), np.float32)
    q_mask[:COLS] = query[None] % COLS == np.arange(COLS)[:, None]
    q_mask[COLS : COLS + BLOCK_ROWS] = query[None] // COLS == np.arange(BLOCK_ROWS)[:, None]
    q_mask[COLS + BLOCK_ROWS] = 1.0
    return k_mask, jnp.asarray(q_mask, BF16)


def head_ones():
    lane = np.arange(PAIR)
    same = (lane[:, None] // HEAD == lane[None] // HEAD) / HEAD
    return jnp.asarray(np.concatenate([same, same], axis=0), BF16)


def local_layer(ctr, side, cot, gain, w_qkv, w_out, head_scale, k_mask, q_mask):
    vmem = pl.BlockSpec(memory_space=pltpu.VMEM)
    return pl.pallas_call(
        layer_kernel,
        grid=(PAIRS,),
        in_specs=[pl.BlockSpec(memory_space=pltpu.SMEM)] + [vmem] * 9,
        out_specs=[vmem] * 5,
        out_shape=[
            jax.ShapeDtypeStruct((ROWS, COLS, WIDTH), BF16),
            jax.ShapeDtypeStruct((EXT_ROWS, COLS, WIDTH), F32),
            jax.ShapeDtypeStruct((EXT_ROWS, 2 * SIDE, WIDTH), BF16),
            jax.ShapeDtypeStruct((WIDTH, 4 * WIDTH), BF16),
            jax.ShapeDtypeStruct((8, WIDTH), F32),
        ],
        scratch_shapes=[
            pltpu.VMEM((EXT_PAD, WIDTH), F32),
            pltpu.VMEM((EXT_PAD, 1), F32),
            pltpu.VMEM((EXT_PAD, WIDTH), BF16),
            pltpu.VMEM((WIDTH, EXT_PAD), BF16),
            pltpu.VMEM((EXT_PAD, WIDTH), F32),
            pltpu.VMEM((EXT_PAD, 3 * PAIR), F32),
            pltpu.VMEM((EXT_PAD, PAIR), F32),
            pltpu.VMEM((EXT_PAD, PAIR), F32),
            pltpu.VMEM((EXT_PAD, PAIR), BF16),
            pltpu.VMEM((EXT_PAD, PAIR), BF16),
            pltpu.VMEM((EXT_PAD, 2 * PAIR), F32),
            pltpu.VMEM((EXT_PAD, 3 * PAIR), F32),
            pltpu.VMEM((WIDTH, WIDTH), BF16),
            pltpu.VMEM((WIDTH, WIDTH), BF16),
        ],
        compiler_params=pltpu.CompilerParams(vmem_limit_bytes=48 * 1024 * 1024),
        cost_estimate=pl.CostEstimate(flops=8 * 10**9, bytes_accessed=8 * 10**6, transcendentals=10**6),
        name="layer",
    )(head_scale, ctr, side, cot, gain, w_qkv, w_out, k_mask, q_mask, head_ones())


def shifted(value, axis, up):
    count = lax.axis_size(axis)
    pairs = [(i, i + 1) for i in range(count - 1)]
    return lax.ppermute(value, axis, pairs if up else [(b, a) for a, b in pairs])


def body(tokens, norm_gain, w_qkv, w_out, head_scale, cotangent):
    n_row, n_col = lax.axis_size(ROW), lax.axis_size(COL)
    row_start = lax.axis_index(ROW) * ROWS
    col_start = lax.axis_index(COL) * COLS
    k_mask, q_mask = masks(row_start, col_start, n_row * ROWS, n_col * COLS)
    above = shifted(tokens[-MARGIN:], ROW, True)
    below = shifted(tokens[:MARGIN], ROW, False)
    ctr = jnp.concatenate([above, tokens, below], axis=0)
    left = shifted(ctr[:, -SIDE:], COL, True)
    right = shifted(ctr[:, :SIDE], COL, False)
    side = jnp.concatenate([right, left], axis=1)
    layer_out, d_ctr, d_side, d_w, small = local_layer(
        ctr, side, cotangent.reshape(ROWS * COLS, WIDTH), norm_gain[None], w_qkv, w_out,
        head_scale, k_mask, q_mask,
    )
    d_tokens = fold(d_ctr, d_side, cotangent)
    d_w_qkv, d_w_out, d_gain, d_scale = reduce_all(d_w, small)
    factor = F32(1.0 / math.sqrt(n_row * ROWS * n_col * COLS))
    return layer_out, d_tokens, d_gain * factor, d_scale * factor, d_w_qkv * factor, d_w_out * factor


ROW = ("y", "x_lo")
COL = ("x_hi", "z", "core")
CHIPS = ("y", "x_lo", "x_hi", "z")


def fold(d_ctr, d_side, cotangent):
    from_left = shifted(d_side[:, :MARGIN], COL, True)
    from_right = shifted(d_side[:, SIDE + 1 :], COL, False)
    zeros = jnp.zeros((EXT_ROWS, COLS - 2 * MARGIN, WIDTH), F32)
    mid = d_ctr + jnp.concatenate([from_left.astype(F32), zeros, from_right.astype(F32)], axis=1)
    from_below = shifted(mid[:MARGIN].astype(BF16), ROW, False)
    from_above = shifted(mid[-MARGIN:].astype(BF16), ROW, True)
    zeros = jnp.zeros((ROWS - 2 * MARGIN, COLS, WIDTH), F32)
    rims = jnp.concatenate([from_above.astype(F32), zeros, from_below.astype(F32)], axis=0)
    return (cotangent.astype(F32) + (mid[MARGIN:-MARGIN] + rims)).astype(BF16)


def reduce_all(d_w, small):
    n_row, n_col = lax.axis_size(ROW), lax.axis_size(COL)
    swap = [(0, 1), (1, 0)]
    vec = jnp.concatenate([small[0], small[1, :HEADS]])
    other = lax.ppermute(jnp.stack(split_two(vec)), "core", swap).astype(F32)
    extra = jnp.concatenate(split_two(vec + (other[0] + other[1])))
    extra = jnp.pad(extra, (0, 8 * 256 - extra.shape[0])).reshape(8, 256)
    core = lax.axis_index("core")
    parts = d_w.reshape(n_col // 2, 2, WIDTH // n_col, 4 * WIDTH)
    keep = lax.dynamic_index_in_dim(parts, core, 1, keepdims=False)
    send = lax.dynamic_index_in_dim(parts, 1 - core, 1, keepdims=False)
    got = lax.ppermute(send, "core", swap)
    half = (keep.astype(F32) + got.astype(F32)).astype(BF16)
    half = half.reshape(n_col // 2 * 32, 4 * WIDTH)
    per = 3 * WIDTH // n_row
    per_out = WIDTH // n_row
    qkv = half[:, : 3 * WIDTH].reshape(n_col // 2, 32, n_row, per).transpose(2, 0, 1, 3)
    out = half[:, 3 * WIDTH :].reshape(n_col // 2, 32, n_row, per_out).transpose(2, 0, 1, 3)
    chunk = jnp.concatenate([qkv, out], axis=-1).reshape(n_row * n_col // 2, 32, per + per_out)
    extra = jnp.broadcast_to(extra[None], (n_row * n_col // 2, 8, 256))
    chunk = jnp.concatenate([chunk, extra], axis=1)
    every = lax.all_to_all(chunk, CHIPS, 0, 0)
    total = jnp.sum(every.astype(F32), axis=0)
    vec = total[32:].reshape(-1)
    vec = vec[: WIDTH + HEADS] + vec[WIDTH + HEADS : 2 * (WIDTH + HEADS)]
    return total[:32, :per], total[:32, per:], vec[:WIDTH], vec[WIDTH:]


def solution(mesh):
    fine = Mesh(mesh.devices.reshape(4, 2, 2, 4, 2), ("y", "x_lo", "x_hi", "z", "core"))
    grid = P(ROW, COL, None)
    return jax.shard_map(
        body,
        mesh=fine,
        in_specs=(grid, P(), P(), P(), P(), grid),
        out_specs=(grid, grid, P(), P(), P(COL, ROW), P(COL, ROW)),
        check_vma=False,
    )
```

```python
import functools
import math

import jax
import jax.numpy as jnp
import numpy as np
from jax import lax
from jax.experimental import pallas as pl
from jax.experimental.pallas import tpu as pltpu
from jax.sharding import Mesh
from jax.sharding import PartitionSpec as P

HEAD = 64
HEADS = 8
WINDOW = 7
WIDTH = 512
EPS = 1e-06

MARGIN = WINDOW // 2
ROWS, COLS = 16, 32
SIDE = 4
PITCH = COLS + 2 * SIDE
EXT_ROWS = ROWS + 2 * MARGIN
EXT = EXT_ROWS * PITCH
EXT_PAD = -(-EXT // 128) * 128
BLOCK_ROWS = 4
BLOCKS = ROWS // BLOCK_ROWS
QUERIES = BLOCK_ROWS * COLS
KEY_ROWS = BLOCK_ROWS + 2 * MARGIN
KEYS = KEY_ROWS * PITCH
STEP = BLOCK_ROWS * PITCH
PAIR = 2 * HEAD
PAIRS = HEADS // 2
FAR = -1.0e4
LANES = 128
TAIL = 8
EXTRA = 16
LOG2E = math.log2(math.e)
LN2 = math.log(2.0)

F32 = jnp.float32
BF16 = jnp.bfloat16


def mm(a, b):
    return lax.dot_general(a, b, (((1,), (0,)), ((), ())), preferred_element_type=F32)


def mm_nt(a, b):
    return lax.dot_general(a, b, (((1,), (1,)), ((), ())), preferred_element_type=F32)


def mm_tn(a, b):
    return lax.dot_general(a, b, (((0,), (0,)), ((), ())), preferred_element_type=F32)


def split_two(v):
    high = v.astype(BF16)
    return high, (v - high.astype(F32)).astype(BF16)


def head_mean(v, ones):
    high, low = split_two(v)
    return mm(jnp.concatenate([high, low], axis=1), ones)


def row_of(tokens, above_rows, below_rows, row):
    if row < MARGIN:
        return above_rows[row].astype(F32)
    if row < MARGIN + ROWS:
        return tokens[row - MARGIN].astype(F32)
    return below_rows[row - MARGIN - ROWS].astype(F32)


def layer_kernel(
    total_rows, total_cols,
    place, scale_ref, tokens, above_rows, below_rows, side, gain, k_fixed, q_mask, ones_ref, cot_hbm, w_qkv_hbm, w_out_hbm,
    d_w_keep, d_w_send, d_qkv, attn,
    cot, w_qkv, w_out, sems,
    xhat, nb, nb_t, raw, k_hat, k_inv, kb, vb, d_kv, d_raw, attn_t, k_mask, small, d_w, gain_sum,
):
    for pair in range(PAIRS):
        layer_pair(total_rows, total_cols, pair, place, scale_ref, tokens, above_rows, below_rows, side, gain, k_fixed, q_mask, ones_ref, cot_hbm, w_qkv_hbm, w_out_hbm, d_w_keep, d_w_send, d_qkv, attn, cot, w_qkv, w_out, sems, xhat, nb, nb_t, raw, k_hat, k_inv, kb, vb, d_kv, d_raw, attn_t, k_mask, small, d_w, gain_sum)


def layer_pair(
    total_rows, total_cols, pair, place, scale_ref, tokens, above_rows, below_rows, side, gain, k_fixed, q_mask, ones_ref, cot_hbm, w_qkv_hbm, w_out_hbm, d_w_keep, d_w_send, d_qkv, attn, cot, w_qkv, w_out, sems, xhat, nb, nb_t, raw, k_hat, k_inv, kb, vb, d_kv, d_raw, attn_t, k_mask, small, d_w, gain_sum,
):
    core = place[2]
    half = WIDTH // 2
    at = lambda base: slice(base + pair * PAIR, base + (pair + 1) * PAIR)

    @pl.when(pair == 0)
    def _():
        loads = [
            pltpu.make_async_copy(source, target, sems.at[i])
            for i, (source, target) in enumerate([(w_qkv_hbm, w_qkv), (w_out_hbm, w_out), (cot_hbm, cot)])
        ]
        for load in loads:
            load.start()
        lane_m = lax.broadcasted_iota(jnp.int32, (PITCH, 128), 1)
        col = lax.broadcasted_iota(jnp.int32, (PITCH, 128), 0)
        col = place[1] + jnp.where(col < COLS + SIDE, col, col - PITCH)
        flag = lane_m == COLS + BLOCK_ROWS
        col_far = jnp.where(flag & ((col < 0) | (col >= total_cols)), FAR, 0.0)
        row_far = jnp.where(flag, FAR, 0.0)
        for b in range(BLOCKS):
            for r in range(KEY_ROWS):
                rows = slice(r * PITCH, (r + 1) * PITCH)
                row = place[0] + (b * BLOCK_ROWS + r - MARGIN)
                gone = jnp.where((row < 0) | (row >= total_rows), 1.0, 0.0)
                k_mask[b, rows, :] = k_fixed[rows, :] + col_far + row_far * gone
        xhat[EXT:, :] = jnp.zeros((EXT_PAD - EXT, WIDTH), F32)
        for r in range(EXT_ROWS):
            xhat[r * PITCH : r * PITCH + COLS, :] = row_of(tokens, above_rows, below_rows, r)
            xhat[r * PITCH + COLS : (r + 1) * PITCH, :] = side[r].astype(F32)
        for top in range(0, EXT_PAD, 128):
            rows = slice(top, top + 128)
            x = xhat[rows, :]
            inv = lax.rsqrt(jnp.mean(x * x, axis=-1, keepdims=True) + EPS)
            normed = (x * inv * gain[...]).astype(BF16)
            nb[rows, :] = normed
            nb_t[:, rows] = normed.T
        gain_sum[...] = jnp.zeros((WIDTH, PAIR), F32)
        small[...] = jnp.zeros((8, WIDTH), F32)
        for load in loads:
            load.wait()

    ones = ones_ref[...]
    w_pair = jnp.concatenate([w_qkv[:, at(0)], w_qkv[:, at(WIDTH)], w_qkv[:, at(2 * WIDTH)]], axis=1)
    raw[...] = mm(nb[...], w_pair)
    k_raw = raw[:, PAIR : 2 * PAIR]
    inv = lax.rsqrt(head_mean(k_raw * k_raw, ones) + EPS)
    k_inv[...] = inv
    k_hat[...] = k_raw * inv
    kb[...] = (k_raw * inv).astype(BF16)
    vb[...] = raw[:, 2 * PAIR :].astype(BF16)
    own = [(MARGIN + r) * PITCH for r in range(ROWS)]
    q_raw = jnp.concatenate([raw[o : o + COLS, 0:PAIR] for o in own], axis=0)
    q_inv = lax.rsqrt(head_mean(q_raw * q_raw, ones) + EPS)
    q_hat = q_raw * q_inv
    lane = lax.broadcasted_iota(jnp.int32, (1, PAIR), 1)
    scale = jnp.where(lane < HEAD, scale_ref[2 * pair], scale_ref[2 * pair + 1])
    q_scaled = q_hat * (scale * (LOG2E / HEAD))
    d_attn_t = mm_nt(w_out[at(0), :], cot[...]).astype(BF16)
    first_rows = lax.broadcasted_iota(jnp.int32, (PAIR, QUERIES), 0) < HEAD
    first_lanes = lax.broadcasted_iota(jnp.int32, (QUERIES, PAIR), 1) < HEAD
    d_kv[...] = jnp.zeros((EXT_PAD, 2 * PAIR), F32)

    def beside(v):
        return jnp.concatenate(
            [jnp.where(first_rows, v, 0.0), jnp.where(first_rows, 0.0, v)], axis=1
        ).astype(BF16)

    def above(v):
        return jnp.concatenate(
            [jnp.where(first_lanes, v, 0.0), jnp.where(first_lanes, 0.0, v)], axis=0
        ).astype(BF16)

    def diagonal(v):
        return jnp.concatenate([v[:HEAD, :QUERIES], v[HEAD:, QUERIES:]], axis=0)

    def spread(v):
        return jnp.where(first_rows, v[:, :QUERIES], v[:, QUERIES:])

    every = range(BLOCKS)
    cells = [slice(b * STEP, b * STEP + KEYS) for b in every]
    queries = [slice(b * QUERIES, (b + 1) * QUERIES) for b in every]
    q_nat = [q_scaled[queries[b], :] for b in every]
    weight = []
    for b in every:
        q_all = jnp.concatenate([beside(q_nat[b].T), q_mask[...]], axis=0)
        mask = k_mask[b].astype(BF16)
        weight.append(jnp.exp2(mm(jnp.concatenate([kb[cells[b], :], mask], axis=1), q_all)))
    weight_b = [w.astype(BF16) for w in weight]
    inv_den = [spread(1.0 / jnp.sum(w.astype(F32), axis=0, keepdims=True)) for w in weight_b]
    out_t = [diagonal(mm_tn(vb[cells[b], :], weight_b[b])) * inv_den[b] for b in every]
    d_out_t = [d_attn_t[:, queries[b]].astype(F32) * inv_den[b] for b in every]
    d_weight = [mm(vb[cells[b], :], beside(d_out_t[b])) for b in every]
    delta = []
    for b in every:
        dot_t = d_out_t[b] * out_t[b]
        delta.append(
            jnp.concatenate(
                [jnp.sum(dot_t[:HEAD], axis=0, keepdims=True), jnp.sum(dot_t[HEAD:], axis=0, keepdims=True)],
                axis=1,
            )
        )
    d_values = [mm(weight_b[b], above(d_out_t[b].T)) for b in every]
    d_score = [(weight[b] * (d_weight[b] - delta[b])).astype(BF16) for b in every]
    d_keys = [mm(d_score[b], above(q_nat[b])) for b in every]
    d_q_parts = [diagonal(mm_tn(kb[cells[b], :], d_score[b])).T for b in every]
    for b in every:
        attn_t[at(0), queries[b]] = out_t[b].astype(BF16)
        attn[queries[b], at(0)] = out_t[b].T.astype(BF16)
        d_kv[cells[b], 0:PAIR] += d_keys[b]
        d_kv[cells[b], PAIR:] += d_values[b]

    d_q = jnp.concatenate(d_q_parts, axis=0) * (scale * (1.0 / HEAD))
    dot_q = q_hat * d_q
    by_lane = jnp.sum(dot_q, axis=0, keepdims=True) / scale
    first = jnp.sum(jnp.where(lane < HEAD, by_lane, 0.0), axis=1, keepdims=True)
    second = jnp.sum(jnp.where(lane < HEAD, 0.0, by_lane), axis=1, keepdims=True)
    spot = lax.broadcasted_iota(jnp.int32, (1, WIDTH), 1)
    small[1:2, :] += jnp.where(spot == 2 * pair, first, 0.0) + jnp.where(spot == 2 * pair + 1, second, 0.0)
    d_q_raw = q_inv * (d_q - q_hat * head_mean(dot_q, ones))
    d_raw[:, 0:PAIR] = jnp.zeros((EXT_PAD, PAIR), F32)
    for r, o in enumerate(own):
        d_raw[o : o + COLS, 0:PAIR] = d_q_raw[r * COLS : (r + 1) * COLS, :]
    d_k = d_kv[:, 0:PAIR] * LN2
    k_h = k_hat[...]
    d_raw[:, PAIR : 2 * PAIR] = k_inv[...] * (d_k - k_h * head_mean(k_h * d_k, ones))
    d_raw[:, 2 * PAIR :] = d_kv[:, PAIR:]
    d_raw_b = d_raw[...].astype(BF16)
    d_w_pair = mm(nb_t[...], d_raw_b)
    moved = d_w_pair * w_pair.astype(F32)
    gain_sum[...] += moved[:, :PAIR] + moved[:, PAIR : 2 * PAIR] + moved[:, 2 * PAIR :]
    for part in range(3):
        d_qkv[:, at(part * WIDTH)] = d_raw_b[:, part * PAIR : (part + 1) * PAIR]
        d_w[:, at(part * WIDTH)] = d_w_pair[:, part * PAIR : (part + 1) * PAIR].astype(BF16)

    @pl.when(pair == PAIRS - 1)
    def _():
        d_w[:, 3 * WIDTH :] = mm(attn_t[...], cot[...]).astype(BF16)
        for c in range(WIDTH // 64):
            rows = slice(c * 32, (c + 1) * 32)
            d_w_keep[rows, :] = d_w[pl.ds(pl.multiple_of(c * 64 + 32 * core, 32), 32), :]
            d_w_send[rows, :] = d_w[pl.ds(pl.multiple_of(c * 64 + 32 * (1 - core), 32), 32), :]
        high, low = split_two(gain_sum[...])
        unit = jnp.ones((8, PAIR), BF16)
        d_gain = (mm_nt(unit, high) + mm_nt(unit, low))[0:1] / gain[...]
        vec = jnp.concatenate([d_gain, small[1:2, :]], axis=1)
        high, low = split_two(vec)
        line = jnp.concatenate([high[:, :WIDTH], low[:, :WIDTH], high[:, WIDTH:], low[:, WIDTH:]], axis=1)
        lines = jnp.broadcast_to(line.astype(F32), (EXTRA, 4 * WIDTH)).astype(BF16)
        d_w_keep[half:, :] = lines
        d_w_send[half:, :] = lines


def input_kernel(
    d_qkv, attn, w_qkv, w_out, tokens, above_rows, below_rows, side, gain, layer_out, d_ctr, d_side, xhat, d_norm,
):
    d_norm[...] = mm_nt(d_qkv[...], w_qkv[...])
    mixed = mm(attn[...], w_out[...])
    for r in range(EXT_ROWS):
        rows = slice(r * PITCH, (r + 1) * PITCH)
        xhat[0:COLS, :] = row_of(tokens, above_rows, below_rows, r)
        xhat[COLS:, :] = side[r].astype(F32)
        x = xhat[...]
        inv = lax.rsqrt(jnp.mean(x * x, axis=-1, keepdims=True) + EPS)
        x = x * inv
        d_n = d_norm[rows, :] * gain[...]
        d_x = inv * (d_n - x * jnp.mean(x * d_n, axis=-1, keepdims=True))
        d_ctr[r] = d_x[:COLS]
        d_side[r] = d_x[COLS:].astype(BF16)
    for r in range(ROWS):
        layer_out[r] = (tokens[r].astype(F32) + mixed[r * COLS : (r + 1) * COLS, :]).astype(BF16)


def input_grads(d_qkv, attn, w_qkv, w_out, tokens, above, below, side, gain):
    vmem = pl.BlockSpec(memory_space=pltpu.VMEM)
    return pl.pallas_call(
        input_kernel,
        in_specs=[vmem] * 9,
        out_specs=[vmem] * 3,
        out_shape=[
            jax.ShapeDtypeStruct((ROWS, COLS, WIDTH), BF16),
            jax.ShapeDtypeStruct((EXT_ROWS, COLS, WIDTH), F32),
            jax.ShapeDtypeStruct((EXT_ROWS, 2 * SIDE, WIDTH), BF16),
        ],
        scratch_shapes=[pltpu.VMEM((PITCH, WIDTH), F32), pltpu.VMEM((EXT_PAD, WIDTH), F32)],
        compiler_params=pltpu.CompilerParams(vmem_limit_bytes=24 * 1024 * 1024),
        cost_estimate=pl.CostEstimate(flops=2 * 10**9, bytes_accessed=8 * 10**6, transcendentals=10**3),
        name="inputs",
    )(d_qkv, attn, w_qkv, w_out, tokens, above, below, side, gain)


def masks():
    key = np.arange(KEYS)
    k_row, k_col = key // PITCH, key % PITCH
    k_col = np.where(k_col < COLS + SIDE, k_col, k_col - PITCH)
    near_col = np.abs(k_col[:, None] - np.arange(COLS)[None]) <= MARGIN
    ahead = k_row[:, None] - np.arange(BLOCK_ROWS)[None]
    near_row = (ahead >= 0) & (ahead < WINDOW)
    fixed = np.zeros((KEYS, 128), np.float32)
    fixed[:, :COLS] = np.where(near_col, 0.0, FAR)
    fixed[:, COLS : COLS + BLOCK_ROWS] = np.where(near_row, 0.0, FAR)
    query = np.arange(2 * QUERIES) % QUERIES
    q_mask = np.zeros((128, 2 * QUERIES), np.float32)
    q_mask[:COLS] = query[None] % COLS == np.arange(COLS)[:, None]
    q_mask[COLS : COLS + BLOCK_ROWS] = query[None] // COLS == np.arange(BLOCK_ROWS)[:, None]
    q_mask[COLS + BLOCK_ROWS] = 1.0
    return jnp.asarray(fixed), jnp.asarray(q_mask, BF16)


def head_ones():
    lane = np.arange(PAIR)
    same = (lane[:, None] // HEAD == lane[None] // HEAD) / HEAD
    return jnp.asarray(np.concatenate([same, same], axis=0), BF16)


def local_layer(place, tokens, above, below, side, cot, gain, w_qkv, w_out, head_scale, total_rows, total_cols):
    vmem = pl.BlockSpec(memory_space=pltpu.VMEM)
    smem = pl.BlockSpec(memory_space=pltpu.SMEM)
    k_fixed, q_mask = masks()
    return pl.pallas_call(
        functools.partial(layer_kernel, total_rows, total_cols),
        in_specs=[smem] * 2 + [vmem] * 8 + [pl.BlockSpec(memory_space=pl.ANY)] * 3,
        out_specs=[vmem] * 4,
        out_shape=[
            jax.ShapeDtypeStruct((WIDTH // 2 + EXTRA, 4 * WIDTH), BF16),
            jax.ShapeDtypeStruct((WIDTH // 2 + EXTRA, 4 * WIDTH), BF16),
            jax.ShapeDtypeStruct((EXT_PAD, 3 * WIDTH), BF16),
            jax.ShapeDtypeStruct((ROWS * COLS, WIDTH), BF16),
        ],
        scratch_shapes=[
            pltpu.VMEM((ROWS * COLS, WIDTH), BF16),
            pltpu.VMEM((WIDTH, 3 * WIDTH), BF16),
            pltpu.VMEM((WIDTH, WIDTH), BF16),
            pltpu.SemaphoreType.DMA((3,)),
            pltpu.VMEM((EXT_PAD, WIDTH), F32),
            pltpu.VMEM((EXT_PAD, WIDTH), BF16),
            pltpu.VMEM((WIDTH, EXT_PAD), BF16),
            pltpu.VMEM((EXT_PAD, 3 * PAIR), F32),
            pltpu.VMEM((EXT_PAD, PAIR), F32),
            pltpu.VMEM((EXT_PAD, PAIR), F32),
            pltpu.VMEM((EXT_PAD, PAIR), BF16),
            pltpu.VMEM((EXT_PAD, PAIR), BF16),
            pltpu.VMEM((EXT_PAD, 2 * PAIR), F32),
            pltpu.VMEM((EXT_PAD, 3 * PAIR), F32),
            pltpu.VMEM((WIDTH, WIDTH), BF16),
            pltpu.VMEM((BLOCKS, KEYS, 128), F32),
            pltpu.VMEM((8, WIDTH), F32),
            pltpu.VMEM((WIDTH, 4 * WIDTH), BF16),
            pltpu.VMEM((WIDTH, PAIR), F32),
        ],
        compiler_params=pltpu.CompilerParams(vmem_limit_bytes=30 * 1024 * 1024),
        cost_estimate=pl.CostEstimate(flops=8 * 10**9, bytes_accessed=8 * 10**6, transcendentals=10**6),
        name="layer",
    )(place, head_scale, tokens, above, below, side, gain, k_fixed, q_mask, head_ones(), cot, w_qkv, w_out)


def spread_kernel(n_row, keep, got, chunk):
    per, per_out, groups = 3 * WIDTH // n_row, WIDTH // n_row, WIDTH // 64
    folds = (per + per_out) // LANES
    for c in range(groups):
        rows = slice(c * 32, (c + 1) * 32)
        total = (keep[rows, :].astype(F32) + got[rows, :].astype(F32)).astype(BF16)
        for r in range(n_row):
            both = jnp.concatenate(
                [total[:, r * per : (r + 1) * per], total[:, 3 * WIDTH + r * per_out : 3 * WIDTH + (r + 1) * per_out]],
                axis=1,
            )
            for f in range(folds):
                chunk[r * groups + c, f * 32 : (f + 1) * 32, :] = both[:, f * LANES : (f + 1) * LANES]
    line = keep[WIDTH // 2 :, :].astype(F32) + got[WIDTH // 2 :, :].astype(F32)
    gains = line[:1, :WIDTH] + line[:1, WIDTH : 2 * WIDTH]
    high, low = split_two(line[:1, 2 * WIDTH : 2 * WIDTH + LANES] + line[:1, 3 * WIDTH : 3 * WIDTH + LANES])
    parts = [gains[:, i * LANES : (i + 1) * LANES] for i in range(WIDTH // LANES)]
    parts += [high.astype(F32), low.astype(F32)]
    parts += [jnp.zeros((TAIL - len(parts), LANES), F32)]
    extra = jnp.concatenate(parts, axis=0).astype(BF16)
    for i in range(n_row * groups):
        chunk[i, folds * 32 :, :] = extra


def spread_chunks(keep, got, n_row):
    vmem = pl.BlockSpec(memory_space=pltpu.VMEM)
    rows = 32 * 4 * WIDTH // n_row // LANES + TAIL
    return pl.pallas_call(
        functools.partial(spread_kernel, n_row),
        in_specs=[vmem] * 2,
        out_specs=vmem,
        out_shape=jax.ShapeDtypeStruct((n_row * WIDTH // 64, rows, LANES), BF16),
        compiler_params=pltpu.CompilerParams(vmem_limit_bytes=16 * 1024 * 1024),
        name="spread",
    )(keep, got)


def finish_kernel(factor, every, d_w_qkv, d_w_out, d_gain, d_scale):
    total = every[0].astype(F32)
    for i in range(1, every.shape[0]):
        total += every[i].astype(F32)
    total = total * factor
    per = d_w_qkv.shape[1]
    base = total.shape[0] - TAIL
    both = jnp.concatenate([total[i : i + 32] for i in range(0, base, 32)], axis=1)
    d_w_qkv[...] = both[:, :per]
    d_w_out[...] = both[:, per:]
    lines = WIDTH // LANES
    for i in range(lines):
        d_gain[0:1, i * LANES : (i + 1) * LANES] = total[base + i : base + i + 1]
    d_scale[...] = total[base + lines : base + lines + 1] + total[base + lines + 1 : base + lines + 2]


def finish(every, factor, n_row):
    vmem = pl.BlockSpec(memory_space=pltpu.VMEM)
    return pl.pallas_call(
        functools.partial(finish_kernel, factor),
        in_specs=[vmem],
        out_specs=[vmem] * 4,
        out_shape=[
            jax.ShapeDtypeStruct((32, 3 * WIDTH // n_row), F32),
            jax.ShapeDtypeStruct((32, WIDTH // n_row), F32),
            jax.ShapeDtypeStruct((1, WIDTH), F32),
            jax.ShapeDtypeStruct((1, LANES), F32),
        ],
        compiler_params=pltpu.CompilerParams(vmem_limit_bytes=16 * 1024 * 1024),
        name="finish",
    )(every)


def shifted(value, axis, up):
    count = lax.axis_size(axis)
    return lax.ppermute(value, axis, [(i, (i + (1 if up else -1)) % count) for i in range(count)])


def body(tokens, norm_gain, w_qkv, w_out, head_scale, cotangent):
    n_row, n_col = lax.axis_size(ROW), lax.axis_size(COL)
    place = jnp.stack([lax.axis_index(ROW) * ROWS, lax.axis_index(COL) * COLS, lax.axis_index("core")])
    place = place.astype(jnp.int32)
    above = shifted(tokens[-MARGIN:], ROW, True)
    below = shifted(tokens[:MARGIN], ROW, False)
    edges = [jnp.concatenate([v[:, cut] for v in (above, tokens, below)], axis=0) for cut in (slice(-SIDE, None), slice(0, SIDE))]
    right, left = sideways(*edges)
    side = jnp.concatenate([right, left], axis=1)
    gain = norm_gain[None]
    keep, send, d_qkv, attn = local_layer(
        place, tokens, above, below, side, cotangent.reshape(ROWS * COLS, WIDTH), gain,
        w_qkv, w_out, head_scale, n_row * ROWS, n_col * COLS,
    )
    got = lax.ppermute(send, "core", [(0, 1), (1, 0)])
    chunk = spread_chunks(keep, got, n_row)
    layer_out, d_ctr, d_side = input_grads(d_qkv, attn, w_qkv, w_out, tokens, above, below, side, gain)
    chunk, d_ctr, d_side = lax.optimization_barrier((chunk, d_ctr, d_side))
    every = lax.all_to_all(chunk, CHIPS, 0, 0)
    factor = 1.0 / math.sqrt(n_row * ROWS * n_col * COLS)
    d_w_qkv, d_w_out, d_gain, d_scale = finish(every, factor, n_row)
    d_gain, d_scale = d_gain.reshape(WIDTH), d_scale[0, :HEADS]
    parts = fold(d_ctr, d_side)
    place, d_gain, d_scale = lax.optimization_barrier((place, d_gain, d_scale))
    d_tokens = close(place, cotangent, *parts)
    return layer_out, d_tokens, d_gain, d_scale, d_w_qkv, d_w_out


def sideways(to_right, to_left):
    first = lax.axis_index("core") == 0
    inner = lax.ppermute(jnp.where(first, to_right, to_left), "core", [(0, 1), (1, 0)])
    outer = lax.ppermute(jnp.where(first, to_left, to_right), COL, outer_pairs())
    return jnp.where(first, inner, outer), jnp.where(first, outer, inner)


def outer_pairs(rows_down=None):
    n_row, n_col = lax.axis_size(ROW), lax.axis_size(COL)
    partner = [(c + 1) % n_col if c % 2 else (c - 1) % n_col for c in range(n_col)]
    if rows_down is None:
        return list(enumerate(partner))
    return [
        (r * n_col + c, (r + rows_down) % n_row * n_col + partner[c]) for r in range(n_row) for c in range(n_col)
    ]


ROW = ("y", "x_lo")
COL = ("x_hi", "z", "core")
CHIPS = ("y", "x_lo", "x_hi", "z")


def fold(d_ctr, d_side):
    first = lax.axis_index("core") == 0
    to_right, to_left = d_side[:, :MARGIN], d_side[:, SIDE + 1 :]
    inner = lax.ppermute(jnp.where(first, to_right, to_left), "core", [(0, 1), (1, 0)]).astype(F32)
    edge = jnp.where(first, to_left, to_right)
    outer = lax.ppermute(edge[MARGIN:-MARGIN], COL, outer_pairs())
    outer_low = lax.ppermute(edge[:MARGIN], ROW + COL, outer_pairs(-1))
    outer_high = lax.ppermute(edge[-MARGIN:], ROW + COL, outer_pairs(1))
    gap = jnp.zeros((EXT_ROWS, COLS - 2 * MARGIN, WIDTH), F32)
    none = jnp.zeros_like(inner)
    mid = d_ctr + jnp.concatenate([jnp.where(first, none, inner), gap, jnp.where(first, inner, none)], axis=1)
    from_below = shifted(mid[:MARGIN].astype(BF16), ROW, False)
    from_above = shifted(mid[-MARGIN:].astype(BF16), ROW, True)
    return mid, from_above, from_below, outer, outer_high, outer_low


def close_kernel(place, cotangent, mid, above, below, outer, high, low, d_tokens):
    first = place[2] == 0
    gap = jnp.zeros((COLS - MARGIN, WIDTH), F32)
    for r in range(ROWS):
        total = cotangent[r].astype(F32) + mid[MARGIN + r]
        edge = outer[r].astype(F32)
        if r < MARGIN:
            total = total + above[r].astype(F32)
            edge = edge + high[r].astype(F32)
        if r >= ROWS - MARGIN:
            total = total + below[r - (ROWS - MARGIN)].astype(F32)
            edge = edge + low[r - (ROWS - MARGIN)].astype(F32)
        edge = jnp.where(first, jnp.concatenate([edge, gap], axis=0), jnp.concatenate([gap, edge], axis=0))
        d_tokens[r] = (total + edge).astype(BF16)


def close(place, *parts):
    vmem = pl.BlockSpec(memory_space=pltpu.VMEM)
    return pl.pallas_call(
        close_kernel,
        in_specs=[pl.BlockSpec(memory_space=pltpu.SMEM)] + [vmem] * len(parts),
        out_specs=vmem,
        out_shape=jax.ShapeDtypeStruct((ROWS, COLS, WIDTH), BF16),
        compiler_params=pltpu.CompilerParams(vmem_limit_bytes=16 * 1024 * 1024),
        name="close",
    )(place, *parts)


def solution(mesh):
    fine = Mesh(mesh.devices.reshape(4, 2, 2, 4, 2), ("y", "x_lo", "x_hi", "z", "core"))
    grid = P(ROW, COL, None)
    return jax.shard_map(
        body,
        mesh=fine,
        in_specs=(grid, P(), P(), P(), P(), grid),
        out_specs=(grid, grid, P(), P(), P(COL, ROW), P(COL, ROW)),
        check_vma=False,
    )
```

```python
import functools
import math

import jax
import jax.numpy as jnp
import numpy as np
from jax import lax
from jax.experimental import pallas as pl
from jax.experimental.pallas import tpu as pltpu
from jax.sharding import Mesh
from jax.sharding import PartitionSpec as P

HEAD = 64
HEADS = 8
WINDOW = 7
WIDTH = 512
EPS = 1e-06

MARGIN = WINDOW // 2
ROWS, COLS = 16, 32
SIDE = 4
PITCH = COLS + 2 * SIDE
EXT_ROWS = ROWS + 2 * MARGIN
EXT = EXT_ROWS * PITCH
EXT_PAD = -(-EXT // 128) * 128
BLOCK_ROWS = 4
BLOCKS = ROWS // BLOCK_ROWS
QUERIES = BLOCK_ROWS * COLS
KEY_ROWS = BLOCK_ROWS + 2 * MARGIN
KEYS = KEY_ROWS * PITCH
STEP = BLOCK_ROWS * PITCH
PAIR = 2 * HEAD
PAIRS = HEADS // 2
FAR = -1.0e4
LANES = 128
TAIL = 8
EXTRA = 16
LOG2E = math.log2(math.e)
LN2 = math.log(2.0)

F32 = jnp.float32
BF16 = jnp.bfloat16


def mm(a, b):
    return lax.dot_general(a, b, (((1,), (0,)), ((), ())), preferred_element_type=F32)


def mm_nt(a, b):
    return lax.dot_general(a, b, (((1,), (1,)), ((), ())), preferred_element_type=F32)


def mm_tn(a, b):
    return lax.dot_general(a, b, (((0,), (0,)), ((), ())), preferred_element_type=F32)


def split_two(v):
    high = v.astype(BF16)
    return high, (v - high.astype(F32)).astype(BF16)


def head_mean(v, ones):
    high, low = split_two(v)
    return mm(jnp.concatenate([high, low], axis=1), ones)


def own_kernel(
    total_rows, total_cols,
    place, tokens, gain, k_fixed, ones_ref, w_qkv,
    q_hat, q_inv, k_mask, w_copy,
    nb,
):
    w_copy[...] = w_qkv[...]
    per = 128 // COLS
    for top in range(0, ROWS, per):
        x = jnp.concatenate([tokens[top + i].astype(F32) for i in range(per)], axis=0)
        inv = lax.rsqrt(jnp.mean(x * x, axis=-1, keepdims=True) + EPS)
        nb[top * COLS : top * COLS + 128, :] = (x * inv * gain[...]).astype(BF16)
    ones = ones_ref[...]
    for p in range(PAIRS):
        at = slice(p * PAIR, (p + 1) * PAIR)
        raw = mm(nb[...], w_qkv[:, at])
        inv = lax.rsqrt(head_mean(raw * raw, ones) + EPS)
        q_inv[:, at] = inv
        q_hat[:, at] = raw * inv
    lane = lax.broadcasted_iota(jnp.int32, (PITCH, 128), 1)
    col = lax.broadcasted_iota(jnp.int32, (PITCH, 128), 0)
    col = place[1] + jnp.where(col < COLS + SIDE, col, col - PITCH)
    flag = lane == COLS + BLOCK_ROWS
    col_far = jnp.where(flag & ((col < 0) | (col >= total_cols)), FAR, 0.0)
    row_far = jnp.where(flag, FAR, 0.0)
    for b in range(BLOCKS):
        parts = []
        for r in range(KEY_ROWS):
            row = place[0] + (b * BLOCK_ROWS + r - MARGIN)
            gone = jnp.where((row < 0) | (row >= total_rows), 1.0, 0.0)
            parts.append(k_fixed[r * PITCH : (r + 1) * PITCH, :] + col_far + row_far * gone)
        k_mask[b] = jnp.concatenate(parts, axis=0).astype(BF16)


def own_part(place, tokens, gain, w_qkv, total_rows, total_cols):
    vmem = pl.BlockSpec(memory_space=pltpu.VMEM)
    wide = jax.ShapeDtypeStruct((ROWS * COLS, WIDTH), F32)
    return pl.pallas_call(
        functools.partial(own_kernel, total_rows, total_cols),
        in_specs=[pl.BlockSpec(memory_space=pltpu.SMEM)] + [vmem] * 5,
        out_specs=[vmem] * 4,
        out_shape=[
            wide,
            wide,
            jax.ShapeDtypeStruct((BLOCKS, KEYS, 128), BF16),
            jax.ShapeDtypeStruct((WIDTH, 3 * WIDTH), BF16),
        ],
        scratch_shapes=[pltpu.VMEM((ROWS * COLS, WIDTH), BF16)],
        compiler_params=pltpu.CompilerParams(vmem_limit_bytes=16 * 1024 * 1024),
        cost_estimate=pl.CostEstimate(flops=2 * 10**9, bytes_accessed=8 * 10**6, transcendentals=10**4),
        name="own",
    )(place, tokens, gain, masks()[0], head_ones(), w_qkv)


def row_of(tokens, above_rows, below_rows, row):
    if row < MARGIN:
        return above_rows[row].astype(F32)
    if row < MARGIN + ROWS:
        return tokens[row - MARGIN].astype(F32)
    return below_rows[row - MARGIN - ROWS].astype(F32)


def layer_kernel(
    place, scale_ref, tokens, above_rows, below_rows, side, gain, q_mask, ones_ref, cot, w_out, q_hat_all, q_inv_all, k_mask, w_qkv, d_w_keep, d_w_send, d_qkv, attn, xhat, nb, nb_t, raw, k_hat, k_inv, kb, vb, d_kv, d_raw, attn_t, small, gain_sum,
):
    for pair in range(PAIRS):
        layer_pair(pair, place, scale_ref, tokens, above_rows, below_rows, side, gain, q_mask, ones_ref, cot, w_out, q_hat_all, q_inv_all, k_mask, w_qkv, d_w_keep, d_w_send, d_qkv, attn, xhat, nb, nb_t, raw, k_hat, k_inv, kb, vb, d_kv, d_raw, attn_t, small, gain_sum)


def layer_pair(
    pair, place, scale_ref, tokens, above_rows, below_rows, side, gain, q_mask, ones_ref, cot, w_out, q_hat_all, q_inv_all, k_mask, w_qkv, d_w_keep, d_w_send, d_qkv, attn, xhat, nb, nb_t, raw, k_hat, k_inv, kb, vb, d_kv, d_raw, attn_t, small, gain_sum,
):
    core = place[2]
    half = WIDTH // 2
    at = lambda base: slice(base + pair * PAIR, base + (pair + 1) * PAIR)

    def sort_rows(lanes, value):
        for c in range(WIDTH // 64):
            even, odd = value[c * 64 : c * 64 + 32], value[c * 64 + 32 : c * 64 + 64]
            d_w_keep[c * 32 : (c + 1) * 32, lanes] = jnp.where(core == 0, even, odd)
            d_w_send[c * 32 : (c + 1) * 32, lanes] = jnp.where(core == 0, odd, even)

    @pl.when(pair == 0)
    def _():
        xhat[EXT:, :] = jnp.zeros((EXT_PAD - EXT, WIDTH), F32)
        for r in range(EXT_ROWS):
            xhat[r * PITCH : r * PITCH + COLS, :] = row_of(tokens, above_rows, below_rows, r)
            xhat[r * PITCH + COLS : (r + 1) * PITCH, :] = side[r].astype(F32)
        for top in range(0, EXT_PAD, 128):
            rows = slice(top, top + 128)
            x = xhat[rows, :]
            inv = lax.rsqrt(jnp.mean(x * x, axis=-1, keepdims=True) + EPS)
            normed = (x * inv * gain[...]).astype(BF16)
            nb[rows, :] = normed
            nb_t[:, rows] = normed.T
        gain_sum[...] = jnp.zeros((WIDTH, PAIR), F32)
        small[...] = jnp.zeros((8, WIDTH), F32)

    ones = ones_ref[...]
    w_pair = jnp.concatenate([w_qkv[:, at(0)], w_qkv[:, at(WIDTH)], w_qkv[:, at(2 * WIDTH)]], axis=1)
    raw[...] = mm(nb[...], w_pair[:, PAIR:])
    k_raw = raw[:, :PAIR]
    inv = lax.rsqrt(head_mean(k_raw * k_raw, ones) + EPS)
    k_inv[...] = inv
    k_hat[...] = k_raw * inv
    kb[...] = (k_raw * inv).astype(BF16)
    vb[...] = raw[:, PAIR:].astype(BF16)
    own = [(MARGIN + r) * PITCH for r in range(ROWS)]
    q_inv, q_hat = q_inv_all[:, at(0)], q_hat_all[:, at(0)]
    d_attn_t = mm_nt(w_out[at(0), :], cot[...]).astype(BF16)
    lane = lax.broadcasted_iota(jnp.int32, (1, PAIR), 1)
    scale = jnp.where(lane < HEAD, scale_ref[2 * pair], scale_ref[2 * pair + 1])
    q_scaled = q_hat * (scale * (LOG2E / HEAD))
    first_rows = lax.broadcasted_iota(jnp.int32, (PAIR, QUERIES), 0) < HEAD
    first_lanes = lax.broadcasted_iota(jnp.int32, (QUERIES, PAIR), 1) < HEAD
    d_kv[...] = jnp.zeros((EXT_PAD, 2 * PAIR), F32)

    def beside(v):
        return jnp.concatenate(
            [jnp.where(first_rows, v, 0.0), jnp.where(first_rows, 0.0, v)], axis=1
        ).astype(BF16)

    def above(v):
        return jnp.concatenate(
            [jnp.where(first_lanes, v, 0.0), jnp.where(first_lanes, 0.0, v)], axis=0
        ).astype(BF16)

    def diagonal(v):
        return jnp.concatenate([v[:HEAD, :QUERIES], v[HEAD:, QUERIES:]], axis=0)

    def spread(v):
        return jnp.where(first_rows, v[:, :QUERIES], v[:, QUERIES:])

    every = range(BLOCKS)
    cells = [slice(b * STEP, b * STEP + KEYS) for b in every]
    queries = [slice(b * QUERIES, (b + 1) * QUERIES) for b in every]
    q_nat = [q_scaled[queries[b], :] for b in every]
    weight = []
    for b in every:
        q_all = jnp.concatenate([beside(q_nat[b].T), q_mask[...]], axis=0)
        weight.append(jnp.exp2(mm(jnp.concatenate([kb[cells[b], :], k_mask[b]], axis=1), q_all)))
    weight_b = [w.astype(BF16) for w in weight]
    inv_den = [spread(1.0 / jnp.sum(w.astype(F32), axis=0, keepdims=True)) for w in weight_b]
    out_t = [diagonal(mm_tn(vb[cells[b], :], weight_b[b])) * inv_den[b] for b in every]
    d_out_t = [d_attn_t[:, queries[b]].astype(F32) * inv_den[b] for b in every]
    d_weight = [mm(vb[cells[b], :], beside(d_out_t[b])) for b in every]
    delta = []
    for b in every:
        dot_t = d_out_t[b] * out_t[b]
        delta.append(
            jnp.concatenate(
                [jnp.sum(dot_t[:HEAD], axis=0, keepdims=True), jnp.sum(dot_t[HEAD:], axis=0, keepdims=True)],
                axis=1,
            )
        )
    d_values = [mm(weight_b[b], above(d_out_t[b].T)) for b in every]
    d_score = [(weight[b] * (d_weight[b] - delta[b])).astype(BF16) for b in every]
    d_keys = [mm(d_score[b], above(q_nat[b])) for b in every]
    d_q_parts = [diagonal(mm_tn(kb[cells[b], :], d_score[b])).T for b in every]
    for b in every:
        attn_t[at(0), queries[b]] = out_t[b].astype(BF16)
        attn[queries[b], at(0)] = out_t[b].T.astype(BF16)
        d_kv[cells[b], 0:PAIR] += d_keys[b]
        d_kv[cells[b], PAIR:] += d_values[b]

    d_q = jnp.concatenate(d_q_parts, axis=0) * (scale * (1.0 / HEAD))
    dot_q = q_hat * d_q
    by_lane = jnp.sum(dot_q, axis=0, keepdims=True) / scale
    first = jnp.sum(jnp.where(lane < HEAD, by_lane, 0.0), axis=1, keepdims=True)
    second = jnp.sum(jnp.where(lane < HEAD, 0.0, by_lane), axis=1, keepdims=True)
    spot = lax.broadcasted_iota(jnp.int32, (1, WIDTH), 1)
    small[1:2, :] += jnp.where(spot == 2 * pair, first, 0.0) + jnp.where(spot == 2 * pair + 1, second, 0.0)
    d_q_raw = q_inv * (d_q - q_hat * head_mean(dot_q, ones))
    d_raw[:, 0:PAIR] = jnp.zeros((EXT_PAD, PAIR), F32)
    for r, o in enumerate(own):
        d_raw[o : o + COLS, 0:PAIR] = d_q_raw[r * COLS : (r + 1) * COLS, :]
    d_k = d_kv[:, 0:PAIR] * LN2
    k_h = k_hat[...]
    d_raw[:, PAIR : 2 * PAIR] = k_inv[...] * (d_k - k_h * head_mean(k_h * d_k, ones))
    d_raw[:, 2 * PAIR :] = d_kv[:, PAIR:]
    d_raw_b = d_raw[...].astype(BF16)
    d_w_pair = mm(nb_t[...], d_raw_b)
    moved = d_w_pair * w_pair.astype(F32)
    gain_sum[...] += moved[:, :PAIR] + moved[:, PAIR : 2 * PAIR] + moved[:, 2 * PAIR :]
    for part in range(3):
        d_qkv[:, at(part * WIDTH)] = d_raw_b[:, part * PAIR : (part + 1) * PAIR]
        sort_rows(at(part * WIDTH), d_w_pair[:, part * PAIR : (part + 1) * PAIR].astype(BF16))

    @pl.when(pair == PAIRS - 1)
    def _():
        sort_rows(slice(3 * WIDTH, 4 * WIDTH), mm(attn_t[...], cot[...]).astype(BF16))
        high, low = split_two(gain_sum[...])
        unit = jnp.ones((8, PAIR), BF16)
        d_gain = (mm_nt(unit, high) + mm_nt(unit, low))[0:1] / gain[...]
        vec = jnp.concatenate([d_gain, small[1:2, :]], axis=1)
        high, low = split_two(vec)
        line = jnp.concatenate([high[:, :WIDTH], low[:, :WIDTH], high[:, WIDTH:], low[:, WIDTH:]], axis=1)
        lines = jnp.broadcast_to(line.astype(F32), (EXTRA, 4 * WIDTH)).astype(BF16)
        d_w_keep[half:, :] = lines
        d_w_send[half:, :] = lines


def input_kernel(
    d_qkv, attn, w_qkv, w_out, tokens, above_rows, below_rows, side, gain, layer_out, d_ctr, d_side, xhat, d_norm,
):
    d_norm[...] = mm_nt(d_qkv[...], w_qkv[...])
    mixed = mm(attn[...], w_out[...])
    for r in range(EXT_ROWS):
        rows = slice(r * PITCH, (r + 1) * PITCH)
        xhat[0:COLS, :] = row_of(tokens, above_rows, below_rows, r)
        xhat[COLS:, :] = side[r].astype(F32)
        x = xhat[...]
        inv = lax.rsqrt(jnp.mean(x * x, axis=-1, keepdims=True) + EPS)
        x = x * inv
        d_n = d_norm[rows, :] * gain[...]
        d_x = inv * (d_n - x * jnp.mean(x * d_n, axis=-1, keepdims=True))
        d_ctr[r] = d_x[:COLS]
        d_side[r] = d_x[COLS:].astype(BF16)
    for r in range(ROWS):
        layer_out[r] = (tokens[r].astype(F32) + mixed[r * COLS : (r + 1) * COLS, :]).astype(BF16)


def input_grads(d_qkv, attn, w_qkv, w_out, tokens, above, below, side, gain):
    vmem = pl.BlockSpec(memory_space=pltpu.VMEM)
    return pl.pallas_call(
        input_kernel,
        in_specs=[vmem] * 9,
        out_specs=[vmem] * 3,
        out_shape=[
            jax.ShapeDtypeStruct((ROWS, COLS, WIDTH), BF16),
            jax.ShapeDtypeStruct((EXT_ROWS, COLS, WIDTH), F32),
            jax.ShapeDtypeStruct((EXT_ROWS, 2 * SIDE, WIDTH), BF16),
        ],
        scratch_shapes=[pltpu.VMEM((PITCH, WIDTH), F32), pltpu.VMEM((EXT_PAD, WIDTH), F32)],
        compiler_params=pltpu.CompilerParams(vmem_limit_bytes=24 * 1024 * 1024),
        cost_estimate=pl.CostEstimate(flops=2 * 10**9, bytes_accessed=8 * 10**6, transcendentals=10**3),
        name="inputs",
    )(d_qkv, attn, w_qkv, w_out, tokens, above, below, side, gain)


def masks():
    key = np.arange(KEYS)
    k_row, k_col = key // PITCH, key % PITCH
    k_col = np.where(k_col < COLS + SIDE, k_col, k_col - PITCH)
    near_col = np.abs(k_col[:, None] - np.arange(COLS)[None]) <= MARGIN
    ahead = k_row[:, None] - np.arange(BLOCK_ROWS)[None]
    near_row = (ahead >= 0) & (ahead < WINDOW)
    fixed = np.zeros((KEYS, 128), np.float32)
    fixed[:, :COLS] = np.where(near_col, 0.0, FAR)
    fixed[:, COLS : COLS + BLOCK_ROWS] = np.where(near_row, 0.0, FAR)
    query = np.arange(2 * QUERIES) % QUERIES
    q_mask = np.zeros((128, 2 * QUERIES), np.float32)
    q_mask[:COLS] = query[None] % COLS == np.arange(COLS)[:, None]
    q_mask[COLS : COLS + BLOCK_ROWS] = query[None] // COLS == np.arange(BLOCK_ROWS)[:, None]
    q_mask[COLS + BLOCK_ROWS] = 1.0
    return jnp.asarray(fixed), jnp.asarray(q_mask, BF16)


def head_ones():
    lane = np.arange(PAIR)
    same = (lane[:, None] // HEAD == lane[None] // HEAD) / HEAD
    return jnp.asarray(np.concatenate([same, same], axis=0), BF16)


def local_layer(place, tokens, above, below, side, cot, gain, w_out, own, head_scale):
    vmem = pl.BlockSpec(memory_space=pltpu.VMEM)
    smem = pl.BlockSpec(memory_space=pltpu.SMEM)
    return pl.pallas_call(
        layer_kernel,
        in_specs=[smem] * 2 + [vmem] * 13,
        out_specs=[vmem] * 4,
        out_shape=[
            jax.ShapeDtypeStruct((WIDTH // 2 + EXTRA, 4 * WIDTH), BF16),
            jax.ShapeDtypeStruct((WIDTH // 2 + EXTRA, 4 * WIDTH), BF16),
            jax.ShapeDtypeStruct((EXT_PAD, 3 * WIDTH), BF16),
            jax.ShapeDtypeStruct((ROWS * COLS, WIDTH), BF16),
        ],
        scratch_shapes=[
            pltpu.VMEM((EXT_PAD, WIDTH), F32),
            pltpu.VMEM((EXT_PAD, WIDTH), BF16),
            pltpu.VMEM((WIDTH, EXT_PAD), BF16),
            pltpu.VMEM((EXT_PAD, 2 * PAIR), F32),
            pltpu.VMEM((EXT_PAD, PAIR), F32),
            pltpu.VMEM((EXT_PAD, PAIR), F32),
            pltpu.VMEM((EXT_PAD, PAIR), BF16),
            pltpu.VMEM((EXT_PAD, PAIR), BF16),
            pltpu.VMEM((EXT_PAD, 2 * PAIR), F32),
            pltpu.VMEM((EXT_PAD, 3 * PAIR), F32),
            pltpu.VMEM((WIDTH, WIDTH), BF16),
            pltpu.VMEM((8, WIDTH), F32),
            pltpu.VMEM((WIDTH, PAIR), F32),
        ],
        compiler_params=pltpu.CompilerParams(vmem_limit_bytes=30 * 1024 * 1024),
        cost_estimate=pl.CostEstimate(flops=8 * 10**9, bytes_accessed=8 * 10**6, transcendentals=10**6),
        name="layer",
    )(place, head_scale, tokens, above, below, side, gain, masks()[1], head_ones(), cot, w_out, *own)


def spread_kernel(n_row, keep, got, chunk):
    per, per_out, groups = 3 * WIDTH // n_row, WIDTH // n_row, WIDTH // 64
    folds = (per + per_out) // LANES
    for c in range(groups):
        rows = slice(c * 32, (c + 1) * 32)
        total = (keep[rows, :].astype(F32) + got[rows, :].astype(F32)).astype(BF16)
        for r in range(n_row):
            both = jnp.concatenate(
                [total[:, r * per : (r + 1) * per], total[:, 3 * WIDTH + r * per_out : 3 * WIDTH + (r + 1) * per_out]],
                axis=1,
            )
            for f in range(folds):
                chunk[r * groups + c, f * 32 : (f + 1) * 32, :] = both[:, f * LANES : (f + 1) * LANES]
    line = keep[WIDTH // 2 :, :].astype(F32) + got[WIDTH // 2 :, :].astype(F32)
    gains = line[:1, :WIDTH] + line[:1, WIDTH : 2 * WIDTH]
    high, low = split_two(line[:1, 2 * WIDTH : 2 * WIDTH + LANES] + line[:1, 3 * WIDTH : 3 * WIDTH + LANES])
    parts = [gains[:, i * LANES : (i + 1) * LANES] for i in range(WIDTH // LANES)]
    parts += [high.astype(F32), low.astype(F32)]
    parts += [jnp.zeros((TAIL - len(parts), LANES), F32)]
    extra = jnp.concatenate(parts, axis=0).astype(BF16)
    for i in range(n_row * groups):
        chunk[i, folds * 32 :, :] = extra


def spread_chunks(keep, got, n_row):
    vmem = pl.BlockSpec(memory_space=pltpu.VMEM)
    rows = 32 * 4 * WIDTH // n_row // LANES + TAIL
    return pl.pallas_call(
        functools.partial(spread_kernel, n_row),
        in_specs=[vmem] * 2,
        out_specs=vmem,
        out_shape=jax.ShapeDtypeStruct((n_row * WIDTH // 64, rows, LANES), BF16),
        compiler_params=pltpu.CompilerParams(vmem_limit_bytes=16 * 1024 * 1024),
        name="spread",
    )(keep, got)


def finish_kernel(factor, every, d_w_qkv, d_w_out, d_gain, d_scale):
    total = every[0].astype(F32)
    for i in range(1, every.shape[0]):
        total += every[i].astype(F32)
    total = total * factor
    per = d_w_qkv.shape[1]
    base = total.shape[0] - TAIL
    both = jnp.concatenate([total[i : i + 32] for i in range(0, base, 32)], axis=1)
    d_w_qkv[...] = both[:, :per]
    d_w_out[...] = both[:, per:]
    lines = WIDTH // LANES
    for i in range(lines):
        d_gain[0:1, i * LANES : (i + 1) * LANES] = total[base + i : base + i + 1]
    d_scale[...] = total[base + lines : base + lines + 1] + total[base + lines + 1 : base + lines + 2]


def finish(every, factor, n_row):
    vmem = pl.BlockSpec(memory_space=pltpu.VMEM)
    return pl.pallas_call(
        functools.partial(finish_kernel, factor),
        in_specs=[vmem],
        out_specs=[vmem] * 4,
        out_shape=[
            jax.ShapeDtypeStruct((32, 3 * WIDTH // n_row), F32),
            jax.ShapeDtypeStruct((32, WIDTH // n_row), F32),
            jax.ShapeDtypeStruct((1, WIDTH), F32),
            jax.ShapeDtypeStruct((1, LANES), F32),
        ],
        compiler_params=pltpu.CompilerParams(vmem_limit_bytes=16 * 1024 * 1024),
        name="finish",
    )(every)


def shifted(value, axis, up):
    count = lax.axis_size(axis)
    return lax.ppermute(value, axis, [(i, (i + (1 if up else -1)) % count) for i in range(count)])


def body(tokens, norm_gain, w_qkv, w_out, head_scale, cotangent):
    n_row, n_col = lax.axis_size(ROW), lax.axis_size(COL)
    place = jnp.stack([lax.axis_index(ROW) * ROWS, lax.axis_index(COL) * COLS, lax.axis_index("core")])
    place = place.astype(jnp.int32)
    above = shifted(tokens[-MARGIN:], ROW, True)
    below = shifted(tokens[:MARGIN], ROW, False)
    lefts, rights = cuts(tokens)
    left = jnp.concatenate([above[:, :SIDE], lefts, below[:, :SIDE]], axis=0)
    right = jnp.concatenate([above[:, -SIDE:], rights, below[:, -SIDE:]], axis=0)
    right, left = sideways(right, left)
    side = jnp.concatenate([right, left], axis=1)
    gain = norm_gain[None]
    cot = cotangent.reshape(ROWS * COLS, WIDTH)
    held, above, below = lax.optimization_barrier((place, above, below))
    own = own_part(held, tokens, gain, w_qkv, n_row * ROWS, n_col * COLS)
    keep, send, d_qkv, attn = local_layer(place, tokens, above, below, side, cot, gain, w_out, own, head_scale)
    w_qkv = own[-1]
    got = lax.ppermute(send, "core", [(0, 1), (1, 0)])
    chunk = spread_chunks(keep, got, n_row)
    layer_out, d_ctr, d_side = input_grads(d_qkv, attn, w_qkv, w_out, tokens, above, below, side, gain)
    chunk, d_ctr, d_side = lax.optimization_barrier((chunk, d_ctr, d_side))
    every = lax.all_to_all(chunk, CHIPS, 0, 0)
    factor = 1.0 / math.sqrt(n_row * ROWS * n_col * COLS)
    d_w_qkv, d_w_out, d_gain, d_scale = finish(every, factor, n_row)
    d_gain, d_scale = d_gain.reshape(WIDTH), d_scale[0, :HEADS]
    parts = fold(d_ctr, d_side)
    place, d_gain, d_scale = lax.optimization_barrier((place, d_gain, d_scale))
    d_tokens = close(place, cotangent, *parts)
    return layer_out, d_tokens, d_gain, d_scale, d_w_qkv, d_w_out


def cuts_kernel(tokens, left, right):
    for r in range(ROWS):
        row = tokens[r]
        left[r] = row[:SIDE]
        right[r] = row[COLS - SIDE :]


def cuts(tokens):
    vmem = pl.BlockSpec(memory_space=pltpu.VMEM)
    part = jax.ShapeDtypeStruct((ROWS, SIDE, WIDTH), BF16)
    return pl.pallas_call(
        cuts_kernel,
        in_specs=[vmem],
        out_specs=[vmem] * 2,
        out_shape=[part, part],
        compiler_params=pltpu.CompilerParams(vmem_limit_bytes=8 * 1024 * 1024),
        cost_estimate=pl.CostEstimate(flops=10**10, bytes_accessed=4 * 10**7, transcendentals=0),
        name="cuts",
    )(tokens)


def sideways(to_right, to_left):
    first = lax.axis_index("core") == 0
    inner = lax.ppermute(jnp.where(first, to_right, to_left), "core", [(0, 1), (1, 0)])
    outer = lax.ppermute(jnp.where(first, to_left, to_right), COL, outer_pairs())
    return jnp.where(first, inner, outer), jnp.where(first, outer, inner)


def outer_pairs(rows_down=None):
    n_row, n_col = lax.axis_size(ROW), lax.axis_size(COL)
    partner = [(c + 1) % n_col if c % 2 else (c - 1) % n_col for c in range(n_col)]
    if rows_down is None:
        return list(enumerate(partner))
    return [
        (r * n_col + c, (r + rows_down) % n_row * n_col + partner[c]) for r in range(n_row) for c in range(n_col)
    ]


ROW = ("y", "x_lo")
COL = ("x_hi", "z", "core")
CHIPS = ("y", "x_lo", "x_hi", "z")


def fold(d_ctr, d_side):
    first = lax.axis_index("core") == 0
    to_right, to_left = d_side[:, :MARGIN], d_side[:, SIDE + 1 :]
    inner = lax.ppermute(jnp.where(first, to_right, to_left), "core", [(0, 1), (1, 0)]).astype(F32)
    edge = jnp.where(first, to_left, to_right)
    outer = lax.ppermute(edge[MARGIN:-MARGIN], COL, outer_pairs())
    outer_low = lax.ppermute(edge[:MARGIN], ROW + COL, outer_pairs(-1))
    outer_high = lax.ppermute(edge[-MARGIN:], ROW + COL, outer_pairs(1))
    gap = jnp.zeros((EXT_ROWS, COLS - 2 * MARGIN, WIDTH), F32)
    none = jnp.zeros_like(inner)
    mid = d_ctr + jnp.concatenate([jnp.where(first, none, inner), gap, jnp.where(first, inner, none)], axis=1)
    from_below = shifted(mid[:MARGIN].astype(BF16), ROW, False)
    from_above = shifted(mid[-MARGIN:].astype(BF16), ROW, True)
    return mid, from_above, from_below, outer, outer_high, outer_low


def close_kernel(place, cotangent, mid, above, below, outer, high, low, d_tokens):
    first = place[2] == 0
    gap = jnp.zeros((COLS - MARGIN, WIDTH), F32)
    for r in range(ROWS):
        total = cotangent[r].astype(F32) + mid[MARGIN + r]
        edge = outer[r].astype(F32)
        if r < MARGIN:
            total = total + above[r].astype(F32)
            edge = edge + high[r].astype(F32)
        if r >= ROWS - MARGIN:
            total = total + below[r - (ROWS - MARGIN)].astype(F32)
            edge = edge + low[r - (ROWS - MARGIN)].astype(F32)
        edge = jnp.where(first, jnp.concatenate([edge, gap], axis=0), jnp.concatenate([gap, edge], axis=0))
        d_tokens[r] = (total + edge).astype(BF16)


def close(place, *parts):
    vmem = pl.BlockSpec(memory_space=pltpu.VMEM)
    return pl.pallas_call(
        close_kernel,
        in_specs=[pl.BlockSpec(memory_space=pltpu.SMEM)] + [vmem] * len(parts),
        out_specs=vmem,
        out_shape=jax.ShapeDtypeStruct((ROWS, COLS, WIDTH), BF16),
        compiler_params=pltpu.CompilerParams(vmem_limit_bytes=16 * 1024 * 1024),
        name="close",
    )(place, *parts)


def solution(mesh):
    fine = Mesh(mesh.devices.reshape(4, 2, 2, 4, 2), ("y", "x_lo", "x_hi", "z", "core"))
    grid = P(ROW, COL, None)
    return jax.shard_map(
        body,
        mesh=fine,
        in_specs=(grid, P(), P(), P(), P(), grid),
        out_specs=(grid, grid, P(), P(), P(COL, ROW), P(COL, ROW)),
        check_vma=False,
    )
```

```python
import functools
import math

import jax
import jax.numpy as jnp
import numpy as np
from jax import lax
from jax.experimental import pallas as pl
from jax.experimental.pallas import tpu as pltpu
from jax.sharding import Mesh
from jax.sharding import PartitionSpec as P

HEAD = 64
HEADS = 8
WINDOW = 7
WIDTH = 512
EPS = 1e-06

MARGIN = WINDOW // 2
ROWS, COLS = 16, 32
SIDE = 4
PITCH = COLS + 2 * SIDE
EXT_ROWS = ROWS + 2 * MARGIN
EXT = EXT_ROWS * PITCH
EXT_PAD = -(-EXT // 128) * 128
BLOCK_ROWS = 4
BLOCKS = ROWS // BLOCK_ROWS
QUERIES = BLOCK_ROWS * COLS
KEY_ROWS = BLOCK_ROWS + 2 * MARGIN
KEYS = KEY_ROWS * PITCH
STEP = BLOCK_ROWS * PITCH
PAIR = 2 * HEAD
PAIRS = HEADS // 2
FAR = -1.0e4
LANES = 128
TAIL = 8
EXTRA = 16
LOG2E = math.log2(math.e)
LN2 = math.log(2.0)

F32 = jnp.float32
BF16 = jnp.bfloat16


def mm(a, b):
    return lax.dot_general(a, b, (((1,), (0,)), ((), ())), preferred_element_type=F32)


def mm_nt(a, b):
    return lax.dot_general(a, b, (((1,), (1,)), ((), ())), preferred_element_type=F32)


def mm_tn(a, b):
    return lax.dot_general(a, b, (((0,), (0,)), ((), ())), preferred_element_type=F32)


def split_two(v):
    high = v.astype(BF16)
    return high, (v - high.astype(F32)).astype(BF16)


def head_mean(v, ones):
    high, low = split_two(v)
    return mm(jnp.concatenate([high, low], axis=1), ones)


def own_kernel(
    total_rows, total_cols,
    place, tokens, gain, k_fixed, ones_ref, w_qkv,
    q_hat, q_inv, k_mask,
    nb,
):
    per = 128 // COLS
    for top in range(0, ROWS, per):
        x = jnp.concatenate([tokens[top + i].astype(F32) for i in range(per)], axis=0)
        inv = lax.rsqrt(jnp.mean(x * x, axis=-1, keepdims=True) + EPS)
        nb[top * COLS : top * COLS + 128, :] = (x * inv * gain[...]).astype(BF16)
    ones = ones_ref[...]
    for p in range(PAIRS):
        at = slice(p * PAIR, (p + 1) * PAIR)
        raw = mm(nb[...], w_qkv[:, at])
        inv = lax.rsqrt(head_mean(raw * raw, ones) + EPS)
        q_inv[:, at] = inv
        q_hat[:, at] = raw * inv
    lane = lax.broadcasted_iota(jnp.int32, (PITCH, 128), 1)
    col = lax.broadcasted_iota(jnp.int32, (PITCH, 128), 0)
    col = place[1] + jnp.where(col < COLS + SIDE, col, col - PITCH)
    flag = lane == COLS + BLOCK_ROWS
    col_far = jnp.where(flag & ((col < 0) | (col >= total_cols)), FAR, 0.0)
    row_far = jnp.where(flag, FAR, 0.0)
    for b in range(BLOCKS):
        parts = []
        for r in range(KEY_ROWS):
            row = place[0] + (b * BLOCK_ROWS + r - MARGIN)
            gone = jnp.where((row < 0) | (row >= total_rows), 1.0, 0.0)
            parts.append(k_fixed[r * PITCH : (r + 1) * PITCH, :] + col_far + row_far * gone)
        k_mask[b] = jnp.concatenate(parts, axis=0).astype(BF16)


def own_part(place, tokens, gain, w_qkv, total_rows, total_cols):
    vmem = pl.BlockSpec(memory_space=pltpu.VMEM)
    wide = jax.ShapeDtypeStruct((ROWS * COLS, WIDTH), F32)
    return pl.pallas_call(
        functools.partial(own_kernel, total_rows, total_cols),
        in_specs=[pl.BlockSpec(memory_space=pltpu.SMEM)] + [vmem] * 5,
        out_specs=[vmem] * 3,
        out_shape=[
            wide,
            wide,
            jax.ShapeDtypeStruct((BLOCKS, KEYS, 128), BF16),
        ],
        scratch_shapes=[pltpu.VMEM((ROWS * COLS, WIDTH), BF16)],
        compiler_params=pltpu.CompilerParams(vmem_limit_bytes=16 * 1024 * 1024),
        cost_estimate=pl.CostEstimate(flops=2 * 10**9, bytes_accessed=8 * 10**6, transcendentals=10**4),
        name="own",
    )(place, tokens, gain, masks()[0], head_ones(), w_qkv)


def row_of(tokens, above_rows, below_rows, row):
    if row < MARGIN:
        return above_rows[row].astype(F32)
    if row < MARGIN + ROWS:
        return tokens[row - MARGIN].astype(F32)
    return below_rows[row - MARGIN - ROWS].astype(F32)


def layer_kernel(
    place, scale_ref, tokens, above_rows, below_rows, side, gain, q_mask, ones_ref, cot, w_out, q_hat_all, q_inv_all, k_mask, w_qkv, d_w_keep, d_w_send, d_qkv, attn, xhat, nb, nb_t, raw, k_hat, k_inv, kb, vb, d_kv, d_raw, attn_t, small, gain_sum,
):
    for pair in range(PAIRS):
        layer_pair(pair, place, scale_ref, tokens, above_rows, below_rows, side, gain, q_mask, ones_ref, cot, w_out, q_hat_all, q_inv_all, k_mask, w_qkv, d_w_keep, d_w_send, d_qkv, attn, xhat, nb, nb_t, raw, k_hat, k_inv, kb, vb, d_kv, d_raw, attn_t, small, gain_sum)


def layer_pair(
    pair, place, scale_ref, tokens, above_rows, below_rows, side, gain, q_mask, ones_ref, cot, w_out, q_hat_all, q_inv_all, k_mask, w_qkv, d_w_keep, d_w_send, d_qkv, attn, xhat, nb, nb_t, raw, k_hat, k_inv, kb, vb, d_kv, d_raw, attn_t, small, gain_sum,
):
    core = place[2]
    half = WIDTH // 2
    at = lambda base: slice(base + pair * PAIR, base + (pair + 1) * PAIR)

    def sort_rows(lanes, value):
        for c in range(WIDTH // 64):
            even, odd = value[c * 64 : c * 64 + 32], value[c * 64 + 32 : c * 64 + 64]
            d_w_keep[c * 32 : (c + 1) * 32, lanes] = jnp.where(core == 0, even, odd)
            d_w_send[c * 32 : (c + 1) * 32, lanes] = jnp.where(core == 0, odd, even)

    @pl.when(pair == 0)
    def _():
        xhat[EXT:, :] = jnp.zeros((EXT_PAD - EXT, WIDTH), F32)
        for r in range(EXT_ROWS):
            xhat[r * PITCH : r * PITCH + COLS, :] = row_of(tokens, above_rows, below_rows, r)
            xhat[r * PITCH + COLS : (r + 1) * PITCH, :] = side[r].astype(F32)
        for top in range(0, EXT_PAD, 128):
            rows = slice(top, top + 128)
            x = xhat[rows, :]
            inv = lax.rsqrt(jnp.mean(x * x, axis=-1, keepdims=True) + EPS)
            normed = (x * inv * gain[...]).astype(BF16)
            nb[rows, :] = normed
            nb_t[:, rows] = normed.T
        gain_sum[...] = jnp.zeros((WIDTH, PAIR), F32)
        small[...] = jnp.zeros((8, WIDTH), F32)

    ones = ones_ref[...]
    w_pair = jnp.concatenate([w_qkv[:, at(0)], w_qkv[:, at(WIDTH)], w_qkv[:, at(2 * WIDTH)]], axis=1)
    raw[...] = mm(nb[...], w_pair[:, PAIR:])
    k_raw = raw[:, :PAIR]
    inv = lax.rsqrt(head_mean(k_raw * k_raw, ones) + EPS)
    k_inv[...] = inv
    k_hat[...] = k_raw * inv
    kb[...] = (k_raw * inv).astype(BF16)
    vb[...] = raw[:, PAIR:].astype(BF16)
    own = [(MARGIN + r) * PITCH for r in range(ROWS)]
    q_inv, q_hat = q_inv_all[:, at(0)], q_hat_all[:, at(0)]
    d_attn_t = mm_nt(w_out[at(0), :], cot[...]).astype(BF16)
    lane = lax.broadcasted_iota(jnp.int32, (1, PAIR), 1)
    scale = jnp.where(lane < HEAD, scale_ref[2 * pair], scale_ref[2 * pair + 1])
    q_scaled = q_hat * (scale * (LOG2E / HEAD))
    first_rows = lax.broadcasted_iota(jnp.int32, (PAIR, QUERIES), 0) < HEAD
    first_lanes = lax.broadcasted_iota(jnp.int32, (QUERIES, PAIR), 1) < HEAD
    d_kv[...] = jnp.zeros((EXT_PAD, 2 * PAIR), F32)

    def beside(v):
        return jnp.concatenate(
            [jnp.where(first_rows, v, 0.0), jnp.where(first_rows, 0.0, v)], axis=1
        ).astype(BF16)

    def above(v):
        return jnp.concatenate(
            [jnp.where(first_lanes, v, 0.0), jnp.where(first_lanes, 0.0, v)], axis=0
        ).astype(BF16)

    def diagonal(v):
        return jnp.concatenate([v[:HEAD, :QUERIES], v[HEAD:, QUERIES:]], axis=0)

    def spread(v):
        return jnp.where(first_rows, v[:, :QUERIES], v[:, QUERIES:])

    every = range(BLOCKS)
    cells = [slice(b * STEP, b * STEP + KEYS) for b in every]
    queries = [slice(b * QUERIES, (b + 1) * QUERIES) for b in every]
    q_nat = [q_scaled[queries[b], :] for b in every]
    weight = []
    for b in every:
        q_all = jnp.concatenate([beside(q_nat[b].T), q_mask[...]], axis=0)
        weight.append(jnp.exp2(mm(jnp.concatenate([kb[cells[b], :], k_mask[b]], axis=1), q_all)))
    weight_b = [w.astype(BF16) for w in weight]
    inv_den = [spread(1.0 / jnp.sum(w.astype(F32), axis=0, keepdims=True)) for w in weight_b]
    out_t = [diagonal(mm_tn(vb[cells[b], :], weight_b[b])) * inv_den[b] for b in every]
    d_out_t = [d_attn_t[:, queries[b]].astype(F32) * inv_den[b] for b in every]
    d_weight = [mm(vb[cells[b], :], beside(d_out_t[b])) for b in every]
    delta = []
    for b in every:
        dot_t = d_out_t[b] * out_t[b]
        delta.append(
            jnp.concatenate(
                [jnp.sum(dot_t[:HEAD], axis=0, keepdims=True), jnp.sum(dot_t[HEAD:], axis=0, keepdims=True)],
                axis=1,
            )
        )
    d_values = [mm(weight_b[b], above(d_out_t[b].T)) for b in every]
    d_score = [(weight[b] * (d_weight[b] - delta[b])).astype(BF16) for b in every]
    d_keys = [mm(d_score[b], above(q_nat[b])) for b in every]
    d_q_parts = [diagonal(mm_tn(kb[cells[b], :], d_score[b])).T for b in every]
    for b in every:
        attn_t[at(0), queries[b]] = out_t[b].astype(BF16)
        attn[queries[b], at(0)] = out_t[b].T.astype(BF16)
        d_kv[cells[b], 0:PAIR] += d_keys[b]
        d_kv[cells[b], PAIR:] += d_values[b]

    d_q = jnp.concatenate(d_q_parts, axis=0) * (scale * (1.0 / HEAD))
    dot_q = q_hat * d_q
    by_lane = jnp.sum(dot_q, axis=0, keepdims=True) / scale
    first = jnp.sum(jnp.where(lane < HEAD, by_lane, 0.0), axis=1, keepdims=True)
    second = jnp.sum(jnp.where(lane < HEAD, 0.0, by_lane), axis=1, keepdims=True)
    spot = lax.broadcasted_iota(jnp.int32, (1, WIDTH), 1)
    small[1:2, :] += jnp.where(spot == 2 * pair, first, 0.0) + jnp.where(spot == 2 * pair + 1, second, 0.0)
    d_q_raw = q_inv * (d_q - q_hat * head_mean(dot_q, ones))
    d_raw[:, 0:PAIR] = jnp.zeros((EXT_PAD, PAIR), F32)
    for r, o in enumerate(own):
        d_raw[o : o + COLS, 0:PAIR] = d_q_raw[r * COLS : (r + 1) * COLS, :]
    d_k = d_kv[:, 0:PAIR] * LN2
    k_h = k_hat[...]
    d_raw[:, PAIR : 2 * PAIR] = k_inv[...] * (d_k - k_h * head_mean(k_h * d_k, ones))
    d_raw[:, 2 * PAIR :] = d_kv[:, PAIR:]
    d_raw_b = d_raw[...].astype(BF16)
    d_w_pair = mm(nb_t[...], d_raw_b)
    moved = d_w_pair * w_pair.astype(F32)
    gain_sum[...] += moved[:, :PAIR] + moved[:, PAIR : 2 * PAIR] + moved[:, 2 * PAIR :]
    for part in range(3):
        d_qkv[:, at(part * WIDTH)] = d_raw_b[:, part * PAIR : (part + 1) * PAIR]
        sort_rows(at(part * WIDTH), d_w_pair[:, part * PAIR : (part + 1) * PAIR].astype(BF16))

    @pl.when(pair == PAIRS - 1)
    def _():
        sort_rows(slice(3 * WIDTH, 4 * WIDTH), mm(attn_t[...], cot[...]).astype(BF16))
        high, low = split_two(gain_sum[...])
        unit = jnp.ones((8, PAIR), BF16)
        d_gain = (mm_nt(unit, high) + mm_nt(unit, low))[0:1] / gain[...]
        vec = jnp.concatenate([d_gain, small[1:2, :]], axis=1)
        high, low = split_two(vec)
        line = jnp.concatenate([high[:, :WIDTH], low[:, :WIDTH], high[:, WIDTH:], low[:, WIDTH:]], axis=1)
        lines = jnp.broadcast_to(line.astype(F32), (EXTRA, 4 * WIDTH)).astype(BF16)
        d_w_keep[half:, :] = lines
        d_w_send[half:, :] = lines


def input_kernel(
    place, d_qkv, attn, w_qkv, w_out, tokens, above_rows, below_rows, side, gain, layer_out, d_ctr, inner, outer, low, high, xhat, d_norm,
):
    d_norm[...] = mm_nt(d_qkv[...], w_qkv[...])
    mixed = mm(attn[...], w_out[...])
    for r in range(EXT_ROWS):
        rows = slice(r * PITCH, (r + 1) * PITCH)
        xhat[0:COLS, :] = row_of(tokens, above_rows, below_rows, r)
        xhat[COLS:, :] = side[r].astype(F32)
        x = xhat[...]
        inv = lax.rsqrt(jnp.mean(x * x, axis=-1, keepdims=True) + EPS)
        x = x * inv
        d_n = d_norm[rows, :] * gain[...]
        d_x = inv * (d_n - x * jnp.mean(x * d_n, axis=-1, keepdims=True))
        d_ctr[r] = d_x[:COLS]
        to_right, to_left = d_x[COLS : COLS + MARGIN], d_x[COLS + SIDE + 1 :]
        inner[r] = jnp.where(place[2] == 0, to_right, to_left).astype(BF16)
        edge = jnp.where(place[2] == 0, to_left, to_right).astype(BF16)
        if r < MARGIN:
            low[r] = edge
        elif r < MARGIN + ROWS:
            outer[r - MARGIN] = edge
        else:
            high[r - MARGIN - ROWS] = edge
    for r in range(ROWS):
        layer_out[r] = (tokens[r].astype(F32) + mixed[r * COLS : (r + 1) * COLS, :]).astype(BF16)


def input_grads(place, d_qkv, attn, w_qkv, w_out, tokens, above, below, side, gain):
    vmem = pl.BlockSpec(memory_space=pltpu.VMEM)
    return pl.pallas_call(
        input_kernel,
        in_specs=[pl.BlockSpec(memory_space=pltpu.SMEM)] + [vmem] * 9,
        out_specs=[vmem] * 6,
        out_shape=[
            jax.ShapeDtypeStruct((ROWS, COLS, WIDTH), BF16),
            jax.ShapeDtypeStruct((EXT_ROWS, COLS, WIDTH), F32),
            jax.ShapeDtypeStruct((EXT_ROWS, MARGIN, WIDTH), BF16),
            jax.ShapeDtypeStruct((ROWS, MARGIN, WIDTH), BF16),
            jax.ShapeDtypeStruct((MARGIN, MARGIN, WIDTH), BF16),
            jax.ShapeDtypeStruct((MARGIN, MARGIN, WIDTH), BF16),
        ],
        scratch_shapes=[pltpu.VMEM((PITCH, WIDTH), F32), pltpu.VMEM((EXT_PAD, WIDTH), F32)],
        compiler_params=pltpu.CompilerParams(vmem_limit_bytes=24 * 1024 * 1024),
        cost_estimate=pl.CostEstimate(flops=2 * 10**9, bytes_accessed=8 * 10**6, transcendentals=10**3),
        name="inputs",
    )(place, d_qkv, attn, w_qkv, w_out, tokens, above, below, side, gain)


def masks():
    key = np.arange(KEYS)
    k_row, k_col = key // PITCH, key % PITCH
    k_col = np.where(k_col < COLS + SIDE, k_col, k_col - PITCH)
    near_col = np.abs(k_col[:, None] - np.arange(COLS)[None]) <= MARGIN
    ahead = k_row[:, None] - np.arange(BLOCK_ROWS)[None]
    near_row = (ahead >= 0) & (ahead < WINDOW)
    fixed = np.zeros((KEYS, 128), np.float32)
    fixed[:, :COLS] = np.where(near_col, 0.0, FAR)
    fixed[:, COLS : COLS + BLOCK_ROWS] = np.where(near_row, 0.0, FAR)
    query = np.arange(2 * QUERIES) % QUERIES
    q_mask = np.zeros((128, 2 * QUERIES), np.float32)
    q_mask[:COLS] = query[None] % COLS == np.arange(COLS)[:, None]
    q_mask[COLS : COLS + BLOCK_ROWS] = query[None] // COLS == np.arange(BLOCK_ROWS)[:, None]
    q_mask[COLS + BLOCK_ROWS] = 1.0
    return jnp.asarray(fixed), jnp.asarray(q_mask, BF16)


def head_ones():
    lane = np.arange(PAIR)
    same = (lane[:, None] // HEAD == lane[None] // HEAD) / HEAD
    return jnp.asarray(np.concatenate([same, same], axis=0), BF16)


def local_layer(place, tokens, above, below, side, cot, gain, w_out, own, head_scale):
    vmem = pl.BlockSpec(memory_space=pltpu.VMEM)
    smem = pl.BlockSpec(memory_space=pltpu.SMEM)
    return pl.pallas_call(
        layer_kernel,
        in_specs=[smem] * 2 + [vmem] * 13,
        out_specs=[vmem] * 4,
        out_shape=[
            jax.ShapeDtypeStruct((WIDTH // 2 + EXTRA, 4 * WIDTH), BF16),
            jax.ShapeDtypeStruct((WIDTH // 2 + EXTRA, 4 * WIDTH), BF16),
            jax.ShapeDtypeStruct((EXT_PAD, 3 * WIDTH), BF16),
            jax.ShapeDtypeStruct((ROWS * COLS, WIDTH), BF16),
        ],
        scratch_shapes=[
            pltpu.VMEM((EXT_PAD, WIDTH), F32),
            pltpu.VMEM((EXT_PAD, WIDTH), BF16),
            pltpu.VMEM((WIDTH, EXT_PAD), BF16),
            pltpu.VMEM((EXT_PAD, 2 * PAIR), F32),
            pltpu.VMEM((EXT_PAD, PAIR), F32),
            pltpu.VMEM((EXT_PAD, PAIR), F32),
            pltpu.VMEM((EXT_PAD, PAIR), BF16),
            pltpu.VMEM((EXT_PAD, PAIR), BF16),
            pltpu.VMEM((EXT_PAD, 2 * PAIR), F32),
            pltpu.VMEM((EXT_PAD, 3 * PAIR), F32),
            pltpu.VMEM((WIDTH, WIDTH), BF16),
            pltpu.VMEM((8, WIDTH), F32),
            pltpu.VMEM((WIDTH, PAIR), F32),
        ],
        compiler_params=pltpu.CompilerParams(vmem_limit_bytes=30 * 1024 * 1024),
        cost_estimate=pl.CostEstimate(flops=8 * 10**9, bytes_accessed=8 * 10**6, transcendentals=10**6),
        name="layer",
    )(place, head_scale, tokens, above, below, side, gain, masks()[1], head_ones(), cot, w_out, *own)


def spread_kernel(n_row, keep, got, chunk):
    per, per_out, groups = 3 * WIDTH // n_row, WIDTH // n_row, WIDTH // 64
    folds = (per + per_out) // LANES
    for c in range(groups):
        rows = slice(c * 32, (c + 1) * 32)
        total = (keep[rows, :].astype(F32) + got[rows, :].astype(F32)).astype(BF16)
        for r in range(n_row):
            both = jnp.concatenate(
                [total[:, r * per : (r + 1) * per], total[:, 3 * WIDTH + r * per_out : 3 * WIDTH + (r + 1) * per_out]],
                axis=1,
            )
            for f in range(folds):
                chunk[r * groups + c, f * 32 : (f + 1) * 32, :] = both[:, f * LANES : (f + 1) * LANES]
    line = keep[WIDTH // 2 :, :].astype(F32) + got[WIDTH // 2 :, :].astype(F32)
    gains = line[:1, :WIDTH] + line[:1, WIDTH : 2 * WIDTH]
    high, low = split_two(line[:1, 2 * WIDTH : 2 * WIDTH + LANES] + line[:1, 3 * WIDTH : 3 * WIDTH + LANES])
    parts = [gains[:, i * LANES : (i + 1) * LANES] for i in range(WIDTH // LANES)]
    parts += [high.astype(F32), low.astype(F32)]
    parts += [jnp.zeros((TAIL - len(parts), LANES), F32)]
    extra = jnp.concatenate(parts, axis=0).astype(BF16)
    for i in range(n_row * groups):
        chunk[i, folds * 32 :, :] = extra


def spread_chunks(keep, got, n_row):
    vmem = pl.BlockSpec(memory_space=pltpu.VMEM)
    rows = 32 * 4 * WIDTH // n_row // LANES + TAIL
    return pl.pallas_call(
        functools.partial(spread_kernel, n_row),
        in_specs=[vmem] * 2,
        out_specs=vmem,
        out_shape=jax.ShapeDtypeStruct((n_row * WIDTH // 64, rows, LANES), BF16),
        compiler_params=pltpu.CompilerParams(vmem_limit_bytes=16 * 1024 * 1024),
        name="spread",
    )(keep, got)


def finish_kernel(factor, every, d_w_qkv, d_w_out, d_gain, d_scale):
    total = every[0].astype(F32)
    for i in range(1, every.shape[0]):
        total += every[i].astype(F32)
    total = total * factor
    per = d_w_qkv.shape[1]
    base = total.shape[0] - TAIL
    both = jnp.concatenate([total[i : i + 32] for i in range(0, base, 32)], axis=1)
    d_w_qkv[...] = both[:, :per]
    d_w_out[...] = both[:, per:]
    lines = WIDTH // LANES
    for i in range(lines):
        d_gain[0:1, i * LANES : (i + 1) * LANES] = total[base + i : base + i + 1]
    d_scale[...] = total[base + lines : base + lines + 1] + total[base + lines + 1 : base + lines + 2]


def finish(every, factor, n_row):
    vmem = pl.BlockSpec(memory_space=pltpu.VMEM)
    return pl.pallas_call(
        functools.partial(finish_kernel, factor),
        in_specs=[vmem],
        out_specs=[vmem] * 4,
        out_shape=[
            jax.ShapeDtypeStruct((32, 3 * WIDTH // n_row), F32),
            jax.ShapeDtypeStruct((32, WIDTH // n_row), F32),
            jax.ShapeDtypeStruct((1, WIDTH), F32),
            jax.ShapeDtypeStruct((1, LANES), F32),
        ],
        compiler_params=pltpu.CompilerParams(vmem_limit_bytes=16 * 1024 * 1024),
        name="finish",
    )(every)


def shifted(value, axis, up):
    count = lax.axis_size(axis)
    return lax.ppermute(value, axis, [(i, (i + (1 if up else -1)) % count) for i in range(count)])


def body(tokens, norm_gain, w_qkv, w_out, head_scale, cotangent):
    n_row, n_col = lax.axis_size(ROW), lax.axis_size(COL)
    place = jnp.stack([lax.axis_index(ROW) * ROWS, lax.axis_index(COL) * COLS, lax.axis_index("core")])
    place = place.astype(jnp.int32)
    above = shifted(tokens[-MARGIN:], ROW, True)
    below = shifted(tokens[:MARGIN], ROW, False)
    lefts, rights = cuts(tokens)
    left = jnp.concatenate([above[:, :SIDE], lefts, below[:, :SIDE]], axis=0)
    right = jnp.concatenate([above[:, -SIDE:], rights, below[:, -SIDE:]], axis=0)
    right, left = sideways(right, left)
    side = jnp.concatenate([right, left], axis=1)
    gain = norm_gain[None]
    cot = cotangent.reshape(ROWS * COLS, WIDTH)
    held, above, below = lax.optimization_barrier((place, above, below))
    own = own_part(held, tokens, gain, w_qkv, n_row * ROWS, n_col * COLS)
    keep, send, d_qkv, attn = local_layer(place, tokens, above, below, side, cot, gain, w_out, (*own, w_qkv), head_scale)
    got = lax.ppermute(send, "core", [(0, 1), (1, 0)])
    chunk = spread_chunks(keep, got, n_row)
    layer_out, d_ctr, *sides = input_grads(place, d_qkv, attn, w_qkv, w_out, tokens, above, below, side, gain)
    chunk, d_ctr, sides = lax.optimization_barrier((chunk, d_ctr, sides))
    every = lax.all_to_all(chunk, CHIPS, 0, 0)
    factor = 1.0 / math.sqrt(n_row * ROWS * n_col * COLS)
    d_w_qkv, d_w_out, d_gain, d_scale = finish(every, factor, n_row)
    d_gain, d_scale = d_gain.reshape(WIDTH), d_scale[0, :HEADS]
    parts = fold(d_ctr, *sides)
    place, d_gain, d_scale = lax.optimization_barrier((place, d_gain, d_scale))
    d_tokens = close(place, cotangent, *parts)
    return layer_out, d_tokens, d_gain, d_scale, d_w_qkv, d_w_out


def cuts_kernel(tokens, left, right):
    for r in range(ROWS):
        row = tokens[r]
        left[r] = row[:SIDE]
        right[r] = row[COLS - SIDE :]


def cuts(tokens):
    vmem = pl.BlockSpec(memory_space=pltpu.VMEM)
    part = jax.ShapeDtypeStruct((ROWS, SIDE, WIDTH), BF16)
    return pl.pallas_call(
        cuts_kernel,
        in_specs=[vmem],
        out_specs=[vmem] * 2,
        out_shape=[part, part],
        compiler_params=pltpu.CompilerParams(vmem_limit_bytes=8 * 1024 * 1024),
        cost_estimate=pl.CostEstimate(flops=10**10, bytes_accessed=4 * 10**7, transcendentals=0),
        name="cuts",
    )(tokens)


def sideways(to_right, to_left):
    first = lax.axis_index("core") == 0
    inner = lax.ppermute(jnp.where(first, to_right, to_left), "core", [(0, 1), (1, 0)])
    outer = lax.ppermute(jnp.where(first, to_left, to_right), COL, outer_pairs())
    return jnp.where(first, inner, outer), jnp.where(first, outer, inner)


def outer_pairs(rows_down=None):
    n_row, n_col = lax.axis_size(ROW), lax.axis_size(COL)
    partner = [(c + 1) % n_col if c % 2 else (c - 1) % n_col for c in range(n_col)]
    if rows_down is None:
        return list(enumerate(partner))
    return [
        (r * n_col + c, (r + rows_down) % n_row * n_col + partner[c]) for r in range(n_row) for c in range(n_col)
    ]


ROW = ("y", "x_lo")
COL = ("x_hi", "z", "core")
CHIPS = ("y", "x_lo", "x_hi", "z")


def fold(d_ctr, inner, outer, low, high):
    first = lax.axis_index("core") == 0
    inner = lax.ppermute(inner, "core", [(0, 1), (1, 0)]).astype(F32)
    outer = lax.ppermute(outer, COL, outer_pairs())
    outer_low = lax.ppermute(low, ROW + COL, outer_pairs(-1))
    outer_high = lax.ppermute(high, ROW + COL, outer_pairs(1))
    gap = jnp.zeros((EXT_ROWS, COLS - 2 * MARGIN, WIDTH), F32)
    none = jnp.zeros_like(inner)
    mid = d_ctr + jnp.concatenate([jnp.where(first, none, inner), gap, jnp.where(first, inner, none)], axis=1)
    from_below = shifted(mid[:MARGIN].astype(BF16), ROW, False)
    from_above = shifted(mid[-MARGIN:].astype(BF16), ROW, True)
    return mid, from_above, from_below, outer, outer_high, outer_low


def close_kernel(place, cotangent, mid, above, below, outer, high, low, d_tokens):
    first = place[2] == 0
    gap = jnp.zeros((COLS - MARGIN, WIDTH), F32)
    for r in range(ROWS):
        total = cotangent[r].astype(F32) + mid[MARGIN + r]
        edge = outer[r].astype(F32)
        if r < MARGIN:
            total = total + above[r].astype(F32)
            edge = edge + high[r].astype(F32)
        if r >= ROWS - MARGIN:
            total = total + below[r - (ROWS - MARGIN)].astype(F32)
            edge = edge + low[r - (ROWS - MARGIN)].astype(F32)
        edge = jnp.where(first, jnp.concatenate([edge, gap], axis=0), jnp.concatenate([gap, edge], axis=0))
        d_tokens[r] = (total + edge).astype(BF16)


def close(place, *parts):
    vmem = pl.BlockSpec(memory_space=pltpu.VMEM)
    return pl.pallas_call(
        close_kernel,
        in_specs=[pl.BlockSpec(memory_space=pltpu.SMEM)] + [vmem] * len(parts),
        out_specs=vmem,
        out_shape=jax.ShapeDtypeStruct((ROWS, COLS, WIDTH), BF16),
        compiler_params=pltpu.CompilerParams(vmem_limit_bytes=16 * 1024 * 1024),
        name="close",
    )(place, *parts)


def solution(mesh):
    fine = Mesh(mesh.devices.reshape(4, 2, 2, 4, 2), ("y", "x_lo", "x_hi", "z", "core"))
    grid = P(ROW, COL, None)
    return jax.shard_map(
        body,
        mesh=fine,
        in_specs=(grid, P(), P(), P(), P(), grid),
        out_specs=(grid, grid, P(), P(), P(COL, ROW), P(COL, ROW)),
        check_vma=False,
    )
```
